512 devices in a mesh: reg: 32 (over z, core), lon: 16 (over y, x).
Axes of the slice: x: 4, y: 4, z: 16, core: 2. Of those that a mesh axis runs over, the one named last changes fastest.
Arguments:
- nodes: bfloat16 [1, 65536, 512], P(None, ('reg', 'lon')), may hold values from -6 to 6
- norm_gain: float32 [512], replicated, may hold values from 0.25 to 1.75
- w_qkv: bfloat16 [512, 1536], replicated
- w_out: bfloat16 [512, 512], replicated, may hold values from -0.25 to 0.25
- w_latent: bfloat16 [512, 512], replicated, may hold values from -0.25 to 0.25
- neighbours: int32 [512, 5], P(('reg', 'lon')), may hold values from 0 to 511, as said below
- assignment: int32 [64, 4096], P('reg', 'lon'), may hold values from 0 to 65535, as said below
- psi: float32 [9, 64, 5, 5], P(None, 'reg'), may hold values from -1.2 to 1.2
- w_dec: bfloat16 [9, 512, 84], replicated, may hold values from -0.09375 to 0.09375
Outputs:
- mesh_state: bfloat16 [1, 65536, 512], P(None, ('reg', 'lon'))
- fields: bfloat16 [1, 84, 64, 4096], P(None, None, 'reg', 'lon')
The draws below stay inside these ranges and needn't reach their ends.
Inputs may be any that keep to these rules, and one draw needn't show every extreme that they name: neighbours[b, 0] = b; the other entries of a row are distinct blocks adjacent to b (diagonals included) on the grid of 32 x 16 blocks, where block b has row b // 16 and column b % 16; columns wrap around, rows do not. `assignment`: the node of cell (i, j) lies in block (i // 2) * 16 + j // 256.
All inputs are finite; a program needn't handle non-finite values.
Results may differ from the reference program's by a relative error of at most 0.011.
Values may be sent and summed in bfloat16 or wider, within the bound.
A program may use at most 64 MiB of HBM per device.

```python
import jax
import jax.numpy as jnp
from jax import lax

D = 512
HEADS = 16
HEAD_DIM = 32
CH = 512
C_OUT = 84
NBAS = 9
BLK = 128
KNB = 5
MEMB = 1
LATD = 2
LOND = 256
REGIONS = 32
SECTORS = 16
NBLK = 512
NODES = 65536
LAT = 64
LON = 4096


def draw_w_qkv(key, part):
    key_base = jax.random.fold_in(key, 0)
    base = jax.random.normal(key_base, (D, 3 * D), jnp.float32) * D ** (-0.5)
    return base.astype(jnp.bfloat16)


def draw_neighbours(key, part):
    blocks = jnp.arange(NBLK, dtype=jnp.int32)
    rows = blocks // SECTORS
    cols = blocks % SECTORS
    step_rows = jnp.array([-1, -1, -1, 0, 0, 1, 1, 1], jnp.int32)
    step_cols = jnp.array([-1, 0, 1, -1, 1, -1, 0, 1], jnp.int32)
    near_rows = rows[:, None] + step_rows[None, :]
    near_cols = (cols[:, None] + step_cols[None, :]) % SECTORS
    valid = (near_rows >= 0) & (near_rows < REGIONS)
    slots = jnp.arange(8, dtype=jnp.int32)[None, :]
    scores = jax.random.randint(key, (NBLK, 8), 0, 1024, jnp.int32) * 8 + slots
    scores = jnp.where(valid, scores, 100000 + slots)
    order = jnp.argsort(scores, axis=1, stable=True)[:, :KNB - 1]
    candidates = near_rows * SECTORS + near_cols
    picked = jnp.take_along_axis(candidates, order, axis=1)
    return jnp.concatenate([blocks[:, None], picked], axis=1).astype(jnp.int32)


def draw_assignment(key, part):
    lat_index = jnp.arange(LAT, dtype=jnp.int32)[:, None]
    lon_index = jnp.arange(LON, dtype=jnp.int32)[None, :]
    owner = lat_index // LATD * SECTORS + lon_index // LOND
    offset = jax.random.randint(key, (LAT, LON), 0, BLK, jnp.int32)
    return (owner * BLK + offset).astype(jnp.int32)


def block_scale(stream_key, shape, cuts, least, top_value):
    level, own = 1.0, jax.random.fold_in(stream_key, 6)
    for dim, parts in cuts:
        heights = jnp.exp(jax.random.uniform(jax.random.fold_in(own, dim), (parts,), jnp.float32, least / len(cuts), top_value / len(cuts)))
        level = level * jnp.repeat(heights, shape[dim] // parts).reshape([-1 if axis == dim else 1 for axis in range(len(shape))])
    return level


def noise(stream_key, extent, width, reach, cuts=(), kind=jnp.bfloat16):
    level = block_scale(stream_key, extent, cuts, -0.22, 0.18) if cuts else 1.0
    values = jax.random.normal(stream_key, extent, jnp.float32) * width * level
    return jnp.minimum(jnp.maximum(values, -reach), reach).astype(kind)


def setup_inputs(seed: int = 0) -> dict:
    keys = jax.random.split(jax.random.key(seed), 10)
    return {
        "nodes": noise(keys[0], (MEMB, NODES, D), 1.0, 6.0, ((1, 512),)),
        "norm_gain": jnp.clip(1.0 + 0.15 * jax.random.normal(keys[1], (D,), jnp.float32), 0.25, 1.75),
        "w_qkv": draw_w_qkv(jax.random.fold_in(keys[9], 71), 0),
        "w_out": noise(keys[3], (D, D), D ** -0.5, 0.25),
        "w_latent": noise(keys[4], (D, CH), D ** -0.5, 0.25),
        "neighbours": draw_neighbours(jax.random.fold_in(keys[9], 71), 0),
        "assignment": draw_assignment(jax.random.fold_in(keys[9], 71), 0),
        "psi": noise(keys[7], (NBAS, LAT, 5, 5), 0.2, 1.2, ((1, 32),), jnp.float32),
        "w_dec": noise(keys[8], (NBAS, CH, C_OUT), (NBAS * CH) ** -0.5, 0.09375),
    }


def layer_norm(nodes, gain):
    values = nodes.astype(jnp.float32)
    center = values - lax.optimization_barrier(jnp.mean(values, axis=-1, keepdims=True))
    spread = lax.optimization_barrier(jnp.mean(center * center, axis=-1, keepdims=True))
    return (center * lax.rsqrt(spread + 1e-05) * gain).astype(jnp.bfloat16)

def reference(nodes, norm_gain, w_qkv, w_out, w_latent, neighbours, assignment, psi, w_dec):
    members = nodes.shape[0]
    normed = layer_norm(nodes, norm_gain)
    flat = normed.reshape(-1, D)
    projected = jnp.dot(flat, w_qkv, preferred_element_type=jnp.float32)
    queries = projected[:, :D].astype(jnp.bfloat16).reshape(members, NBLK, BLK, HEADS, HEAD_DIM)
    keyvals = projected[:, D:].astype(jnp.bfloat16).reshape(members, NBLK, BLK, 2 * D)
    scale = 1.0 / HEAD_DIM ** 0.5

    def attend(block):
        query = lax.dynamic_index_in_dim(queries, block, axis=1, keepdims=False)
        listed = lax.dynamic_index_in_dim(neighbours, block, axis=0, keepdims=False)
        chosen = jnp.take(keyvals, listed, axis=1).reshape(members, KNB * BLK, 2 * D)
        key_part = chosen[..., :D].reshape(members, KNB * BLK, HEADS, HEAD_DIM)
        value_part = chosen[..., D:].reshape(members, KNB * BLK, HEADS, HEAD_DIM)
        scores = jnp.einsum('mqhd,mkhd->mhqk', query.astype(jnp.float32), key_part.astype(jnp.float32)) * scale
        top = lax.optimization_barrier(jnp.max(scores, axis=-1, keepdims=True))
        expo = jnp.exp(scores - top)
        total = lax.optimization_barrier(jnp.sum(expo, axis=-1, keepdims=True))
        rounded = lax.optimization_barrier(expo.astype(jnp.bfloat16))
        summed = jnp.einsum('mhqk,mkhd->mhqd', rounded.astype(jnp.float32), value_part.astype(jnp.float32)) / total
        return summed.transpose(0, 2, 1, 3).reshape(members, BLK, D).astype(jnp.bfloat16)
    blocks_out = lax.map(attend, jnp.arange(NBLK, dtype=jnp.int32))
    attended = blocks_out.transpose(1, 0, 2, 3).reshape(members * NODES, D)
    state = (nodes.reshape(-1, D).astype(jnp.float32) + jnp.dot(attended, w_out, preferred_element_type=jnp.float32)).astype(jnp.bfloat16)
    latent = jax.nn.silu(jnp.dot(state, w_latent, preferred_element_type=jnp.float32)).astype(jnp.bfloat16)
    latent = latent.reshape(members, NODES, CH)
    grid = jnp.take(latent, assignment.reshape(-1).astype(jnp.int32), axis=1).reshape(members * LAT * LON, CH)

    def basis_step(total, inputs):
        taps, mixing = inputs
        mixed = jnp.dot(grid, mixing, preferred_element_type=jnp.float32).reshape(members, LAT, LON, C_OUT)
        padded = jnp.pad(mixed, ((0, 0), (2, 2), (0, 0), (0, 0)))
        padded = jnp.concatenate([padded[:, :, -2:], padded, padded[:, :, :2]], axis=2)
        for row_off in range(5):
            for col_off in range(5):
                total = total + taps[:, row_off, col_off][None, :, None, None] * padded[:, row_off:row_off + LAT, col_off:col_off + LON]
        return (total, None)
    start = jnp.zeros((members, LAT, LON, C_OUT), jnp.float32)
    total, unused = lax.scan(basis_step, start, (psi, w_dec))
    fields = total.transpose(0, 3, 1, 2).astype(jnp.bfloat16)
    return (state.reshape(members, NODES, D), fields)
```

```python
import functools
import math

import jax
import jax.numpy as jnp
from jax import lax
from jax.experimental import pallas as pl
from jax.experimental.pallas import tpu as pltpu
from jax.sharding import PartitionSpec as P

MESH = pl.DeviceIdType.MESH
F32, BF16 = jnp.float32, jnp.bfloat16
HEADS = 16
CHUNKS = 2
BLK, D = 128, 512
COLS = 256
NBAS, OUT, OUTP = 9, 84, 96
NT = (((1,), (1,)), ((), ()))

OWN, LEFT, RIGHT, UP, DOWN, UL, UR, DL, DR = range(9)
STEPS = [(0, 0), (0, -1), (0, 1), (-1, 0), (1, 0), (-1, -1), (-1, 1), (1, -1), (1, 1)]
CODE = [(r + 1) * 3 + c + 1 for r, c in STEPS]

C_UP, C_DOWN, C_AUP, C_ADOWN, C_LUP, C_LDOWN, C_EL, C_ER, C_HUP, C_HDOWN = range(10)
C_LON = 10
C_DIAG = C_LON + 2 * CHUNKS
N_COPIES = C_DIAG + 4 * CHUNKS


def taps_of(blk, i):
    found = []
    for r in range(2):
        a = 2 * (blk - 1) + r - i
        if -2 <= a <= 2:
            found += [(r, e, (i * 5 + a + 2) * 5 + e) for e in range(5)]
    return found


def kernel(
    n_reg, n_lon,
    nodes_h, gain_h, wqkv_h, wout_h, wlat_h, nbr_h, asg_h, psi_h, wdec_h,
    state_o, fields_o,
    xs, gain, wqkv, wout, wlat, nbr, asg, psi, wdec, wtp,
    slots, qb, kb, vb, att, lat, edge, edges_in, halo, onehot_e,
    hot, splat, sel, hmask, hsel,
    load_sem, send_sem, recv_sem,
):
    reg, lon = lax.axis_index("reg"), lax.axis_index("lon")
    up = (lax.rem(reg + n_reg - 1, n_reg), lon)
    down = (lax.rem(reg + 1, n_reg), lon)
    left = (reg, lax.rem(lon + n_lon - 1, n_lon))
    right = (reg, lax.rem(lon + 1, n_lon))

    barrier = pltpu.get_barrier_semaphore()
    for where in (up, down, left, right):
        pl.semaphore_signal(barrier, inc=1, device_id=where, device_id_type=MESH)

    loads = [
        pltpu.make_async_copy(src, dst, load_sem.at[k])
        for k, (src, dst) in enumerate(
            [(nodes_h, xs), (gain_h, gain), (asg_h, asg.at[1]), (psi_h, psi), (nbr_h, nbr),
             (wqkv_h, wqkv), (wdec_h, wdec), (wout_h, wout), (wlat_h, wlat)]
        )
    ]
    for load in loads:
        load.start()

    def remote(k, src, dst, to):
        return pltpu.make_async_remote_copy(
            src_ref=src, dst_ref=dst, send_sem=send_sem.at[k], recv_sem=recv_sem.at[k],
            device_id=to, device_id_type=MESH,
        )

    loads[0].wait()
    loads[1].wait()
    values = xs[...].astype(F32)
    center = values - jnp.mean(values, axis=-1, keepdims=True)
    spread = jnp.mean(center * center, axis=-1, keepdims=True)
    slots[OWN] = (center * lax.rsqrt(spread + 1e-05) * gain[...]).astype(BF16)
    loads[2].wait()

    pl.semaphore_wait(barrier, 4)

    rows = BLK // CHUNKS
    copies = {}
    for c in range(CHUNKS):
        part = pl.ds(c * rows, rows)
        for side, (to, slot) in enumerate(((left, RIGHT), (right, LEFT))):
            k = C_LON + 2 * c + side
            copies[k] = remote(k, slots.at[OWN, part], slots.at[slot, part], to)
            copies[k].start()
    copies[C_UP] = remote(C_UP, slots.at[OWN], slots.at[DOWN], up)
    copies[C_DOWN] = remote(C_DOWN, slots.at[OWN], slots.at[UP], down)
    copies[C_AUP] = remote(C_AUP, asg.at[1], asg.at[2], up)
    copies[C_ADOWN] = remote(C_ADOWN, asg.at[1], asg.at[0], down)
    for k in (C_UP, C_DOWN, C_AUP, C_ADOWN):
        copies[k].start()

    def relay(c):
        part = pl.ds(c * rows, rows)
        for side, (slot, to_up, to_down) in enumerate(((RIGHT, DR, UR), (LEFT, DL, UL))):
            copies[C_LON + 2 * c + side].wait_recv()
            for v, (to, there) in enumerate(((up, to_up), (down, to_down))):
                k = C_DIAG + 4 * c + 2 * side + v
                copies[k] = remote(k, slots.at[slot, part], slots.at[there, part], to)
                copies[k].start()

    loads[3].wait()
    loads[4].wait()

    def spread_taps(k, _):
        i, a, e = k // 25, (k // 5) % 5, k % 5
        row = 2 * reg + i + a - 2
        inside = jnp.logical_and(row >= 0, row < 2 * n_reg)
        for b in range(NBAS):
            value = jnp.where(inside, psi[a, e, i, b], 0.0)
            splat[k * NBAS + b] = jnp.full((16, 128), value, F32).astype(BF16)
        return 0

    lax.fori_loop(0, 50, spread_taps, 0)

    lane = lax.broadcasted_iota(jnp.int32, (8, COLS), 1)
    node = lax.broadcasted_iota(jnp.int32, (BLK, COLS), 0)

    def one_hots(blk):
        for r in range(2):
            local = jnp.broadcast_to(asg[blk, r : r + 1, :] & (BLK - 1), (8, COLS))
            for e in range(5):
                s = e - 2
                moved = pltpu.roll(local, (-s) % COLS, 1) if s else local
                if s < 0:
                    moved = jnp.where(lane < -s, -1, moved)
                if s > 0:
                    moved = jnp.where(lane >= COLS - s, -1, moved)
                tall = jnp.concatenate([moved] * (BLK // 8), axis=0)
                hot[blk, r * 5 + e] = jnp.where(node == tall, 1.0, 0.0).astype(BF16)

    def selections(blk):
        for i in range(2):
            taps = taps_of(blk, i)

            def some(n, _, i=i, taps=taps):
                at = pl.multiple_of(n * 32, 32)
                hots = [hot[blk, r * 5 + e, pl.ds(at, 32), :] for r, e, _ in taps]
                for b in range(NBAS):
                    total = None
                    for h, (_, _, k) in zip(hots, taps, strict=True):
                        tap = splat[k * NBAS + b]
                        tap = jnp.concatenate([tap, tap], axis=0)
                        tap = jnp.concatenate([tap, tap], axis=1)
                        total = tap * h if total is None else total + tap * h
                    sel[blk, pl.ds(b * BLK + at, 32), pl.ds(i * COLS, COLS)] = total
                return 0

            lax.fori_loop(0, BLK // 32, some, 0)

    loads[5].wait()
    scale = math.log2(math.e) / math.sqrt(D // HEADS)
    projected = jnp.dot(slots[OWN], wqkv[...], preferred_element_type=F32)
    qb[...] = (projected[:, :D] * scale).astype(BF16)
    kb[CODE[OWN]] = projected[:, D : 2 * D].astype(BF16)
    vb[CODE[OWN]] = projected[:, 2 * D :].astype(BF16)

    def keys_values(first, count):
        x = slots[first : first + count].reshape(count * BLK, D)
        kv = jnp.dot(x, wqkv[:, D:], preferred_element_type=F32).astype(BF16)
        for n in range(count):
            kb[CODE[first + n]] = kv[n * BLK : (n + 1) * BLK, :D]
            vb[CODE[first + n]] = kv[n * BLK : (n + 1) * BLK, D:]

    one_hots(1)
    relay(0)
    selections(1)
    relay(1)
    keys_values(LEFT, 2)
    copies[C_AUP].wait_recv()
    copies[C_ADOWN].wait_recv()
    one_hots(0)
    one_hots(2)
    selections(0)
    copies[C_UP].wait_recv()
    copies[C_DOWN].wait_recv()
    keys_values(UP, 2)
    selections(2)

    loads[6].wait()
    for b in range(NBAS):
        wtp[pl.ds(b * OUTP, OUTP)] = jnp.concatenate(
            [wdec[b], jnp.zeros((OUTP - OUT, D), BF16)], axis=0
        )

    s_id = lax.broadcasted_iota(jnp.int32, (48, 128), 0)
    l_id = lax.broadcasted_iota(jnp.int32, (48, 128), 1)
    within = s_id % 16
    cell_row = jnp.where(s_id < 16, 0, jnp.where(s_id < 32, -2, 2)) + (within % 4) // 2
    cell_col = jnp.where(within < 4, COLS, -2) + within % 2
    out_col = jnp.where(l_id < 2, l_id, l_id + 128)
    usable = jnp.logical_and(within < 8, jnp.logical_or(l_id < 2, l_id >= 126))
    col_step = jnp.where(usable, cell_col - out_col, 100)
    for i in range(2):
        for a in range(5):
            for e in range(5):
                match = jnp.logical_and(cell_row - i == a - 2, col_step == e - 2)
                hmask[(i * 5 + a) * 5 + e] = jnp.where(match, 1.0, 0.0).astype(BF16)

    def halo_taps(b, _):
        for i in range(2):
            total = None
            for k in range(25):
                tap = splat[(i * 25 + k) * NBAS + b]
                tap = jnp.concatenate([tap] * 3, axis=0)
                term = tap * hmask[i * 25 + k]
                total = term if total is None else total + term
            at = pl.multiple_of(b * 128, 128)
            hsel[pl.ds(at, 48), pl.ds(i * 128, 128)] = total
            hsel[pl.ds(at + 48, 80), pl.ds(i * 128, 128)] = jnp.zeros((80, 128), BF16)
        return 0

    lax.fori_loop(0, NBAS, halo_taps, 0)
    halo[3] = jnp.zeros((16, D), BF16)

    own = asg[1] & (BLK - 1)
    lane1 = lax.broadcasted_iota(jnp.int32, (8, 128), 1)
    marks = jnp.full((8, 128), -1, jnp.int32)
    for r in range(2):
        for side in range(2):
            piece = jnp.broadcast_to(own[r : r + 1, side * 128 : side * 128 + 128], (8, 128))
            first, source = 4 * side + 2 * r, 126 * side
            moved = pltpu.roll(piece, (first - source) % 128, 1) if first != source else piece
            marks = jnp.where(jnp.logical_and(lane1 >= first, lane1 < first + 2), moved, marks)
    tall = jnp.concatenate([marks] * (BLK // 8), axis=0)
    hits = jnp.where(node[:, :128] == tall, 1.0, 0.0)
    onehot_e[...] = jnp.transpose(hits)[:16].astype(BF16)

    for c in range(CHUNKS):
        for n in range(4):
            copies[C_DIAG + 4 * c + n].wait_recv()
    keys_values(UL, 4)

    slot = []
    for n in range(5):
        there = nbr[0, n]
        row_step = there // n_lon - reg
        col_step = lax.rem(there % n_lon - lon + 1 + n_lon, n_lon) - 1
        code = (row_step + 1) * 3 + col_step + 1
        slot.append(jnp.clip(code, 0, 8))
    head_lane = lax.broadcasted_iota(jnp.int32, (BLK, 128), 1) // 32
    ones = jnp.ones((5 * BLK, 128), BF16)
    zero = jnp.zeros((BLK, 128), BF16)
    for g in range(4):
        part = pl.ds(g * 128, 128)
        keys = jnp.concatenate([kb[s, :, part] for s in slot], axis=0)
        vals = jnp.concatenate([vb[s, :, part] for s in slot], axis=0)
        q = qb[:, part]
        wide = jnp.concatenate([jnp.where(head_lane == h, q, zero) for h in range(4)], axis=0)
        scores = lax.dot_general(wide, keys, NT, preferred_element_type=F32)
        top = jnp.max(scores, axis=-1, keepdims=True)
        weights = jnp.exp2(scores - top).astype(BF16)
        summed = jnp.dot(
            weights, jnp.concatenate([vals, ones], axis=1), preferred_element_type=F32
        )
        num, den = summed[:BLK, :128], summed[:BLK, 128:]
        for h in range(1, 4):
            mine = head_lane == h
            num = jnp.where(mine, summed[h * BLK : (h + 1) * BLK, :128], num)
            den = jnp.where(mine, summed[h * BLK : (h + 1) * BLK, 128:], den)
        att[:, part] = (num / den).astype(BF16)

    loads[7].wait()
    loads[8].wait()
    state = (
        xs[...].astype(F32) + jnp.dot(att[...], wout[...], preferred_element_type=F32)
    ).astype(BF16)
    state_o[...] = state
    v = jnp.dot(state, wlat[...], preferred_element_type=F32)
    lat[1] = (v / (1.0 + jnp.exp(-v))).astype(BF16)

    copies[C_LUP] = remote(C_LUP, lat.at[1], lat.at[2], up)
    copies[C_LDOWN] = remote(C_LDOWN, lat.at[1], lat.at[0], down)
    copies[C_LUP].start()
    copies[C_LDOWN].start()
    edge[...] = jnp.dot(onehot_e[...], lat[1], preferred_element_type=F32).astype(BF16)
    copies[C_EL] = remote(C_EL, edge, edges_in.at[0], left)
    copies[C_ER] = remote(C_ER, edge, edges_in.at[1], right)
    copies[C_EL].start()
    copies[C_ER].start()

    def mixed(nodes_in):
        return lax.dot_general(wtp[...], nodes_in, NT, preferred_element_type=F32).astype(BF16)

    def decode(blk):
        z = mixed(lat[blk])
        z = jnp.concatenate([z[b * OUTP : (b + 1) * OUTP] for b in range(NBAS)], axis=1)
        return jnp.dot(z, sel[blk], preferred_element_type=F32)

    total = decode(1)

    copies[C_EL].wait_recv()
    copies[C_ER].wait_recv()
    first4 = lax.broadcasted_iota(jnp.int32, (16, D), 0) < 4
    halo[0] = jnp.where(first4, edges_in[0].astype(F32), edges_in[1].astype(F32)).astype(BF16)
    copies[C_HUP] = remote(C_HUP, halo.at[0], halo.at[2], up)
    copies[C_HDOWN] = remote(C_HDOWN, halo.at[0], halo.at[1], down)
    copies[C_HUP].start()
    copies[C_HDOWN].start()

    copies[C_LUP].wait_recv()
    total += decode(2)
    copies[C_LDOWN].wait_recv()
    total += decode(0)
    copies[C_HUP].wait_recv()
    copies[C_HDOWN].wait_recv()
    z = mixed(jnp.concatenate([halo[0], halo[1], halo[2]] + [halo[3]] * 5, axis=0))
    z = jnp.concatenate([z[b * OUTP : (b + 1) * OUTP] for b in range(NBAS)], axis=1)
    sides = jnp.dot(z, hsel[...], preferred_element_type=F32)
    lane2 = lax.broadcasted_iota(jnp.int32, (OUTP, 128), 1)
    for i in range(2):
        side = sides[:, i * 128 : (i + 1) * 128]
        at_left = jnp.where(lane2 < 2, side, 0.0)
        at_right = jnp.where(lane2 >= 126, side, 0.0)
        whole = total[:, i * COLS : (i + 1) * COLS] + jnp.concatenate([at_left, at_right], axis=1)
        fields_o[i] = whole[:OUT].astype(BF16)

    for copy in copies.values():
        copy.wait_send()


def shards(sizes, nodes, norm_gain, w_qkv, w_out, w_latent, neighbours, assignment, psi, w_dec):
    anywhere = pl.BlockSpec(memory_space=pl.ANY)
    vmem = pl.BlockSpec(memory_space=pltpu.VMEM)
    state, fields = pl.pallas_call(
        functools.partial(kernel, *sizes),
        out_shape=(
            jax.ShapeDtypeStruct((BLK, D), BF16),
            jax.ShapeDtypeStruct((2, OUT, COLS), BF16),
        ),
        in_specs=[anywhere] * 9,
        out_specs=(vmem, vmem),
        scratch_shapes=[
            pltpu.VMEM((BLK, D), BF16),
            pltpu.VMEM((1, D), F32),
            pltpu.VMEM((D, 3 * D), BF16),
            pltpu.VMEM((D, D), BF16),
            pltpu.VMEM((D, D), BF16),
            pltpu.SMEM((1, 5), jnp.int32),
            pltpu.VMEM((3, 2, COLS), jnp.int32),
            pltpu.SMEM((5, 5, 2, NBAS), F32),
            pltpu.VMEM((NBAS, OUT, D), BF16),
            pltpu.VMEM((NBAS * OUTP, D), BF16),
            pltpu.VMEM((9, BLK, D), BF16),
            pltpu.VMEM((BLK, D), BF16),
            pltpu.VMEM((9, BLK, D), BF16),
            pltpu.VMEM((9, BLK, D), BF16),
            pltpu.VMEM((BLK, D), BF16),
            pltpu.VMEM((3, BLK, D), BF16),
            pltpu.VMEM((16, D), BF16),
            pltpu.VMEM((2, 16, D), BF16),
            pltpu.VMEM((4, 16, D), BF16),
            pltpu.VMEM((16, 128), BF16),
            pltpu.VMEM((3, 10, BLK, COLS), BF16),
            pltpu.VMEM((50 * NBAS, 16, 128), BF16),
            pltpu.VMEM((3, NBAS * BLK, 2 * COLS), BF16),
            pltpu.VMEM((50, 48, 128), BF16),
            pltpu.VMEM((NBAS * 128, 256), BF16),
            pltpu.SemaphoreType.DMA((9,)),
            pltpu.SemaphoreType.DMA((N_COPIES,)),
            pltpu.SemaphoreType.DMA((N_COPIES,)),
        ],
        compiler_params=pltpu.CompilerParams(
            collective_id=0, has_side_effects=True, vmem_limit_bytes=56 * 2**20
        ),
    )(
        nodes[0], norm_gain[None], w_qkv, w_out, w_latent, neighbours, assignment,
        psi.transpose(2, 3, 1, 0), w_dec.transpose(0, 2, 1),
    )
    return state[None], fields.transpose(1, 0, 2)[None]


def solution(mesh):
    sizes = (mesh.shape["reg"], mesh.shape["lon"])
    in_specs = (
        P(None, ("reg", "lon"), None),
        P(),
        P(),
        P(),
        P(),
        P(("reg", "lon"), None),
        P("reg", "lon"),
        P(None, "reg", None, None),
        P(),
    )
    out_specs = (P(None, ("reg", "lon"), None), P(None, None, "reg", "lon"))
    return jax.shard_map(
        functools.partial(shards, sizes),
        mesh=mesh,
        in_specs=in_specs,
        out_specs=out_specs,
        check_vma=False,
    )
```

```python
import functools
import math

import jax
import jax.numpy as jnp
from jax import lax
from jax.experimental import pallas as pl
from jax.experimental.pallas import tpu as pltpu
from jax.sharding import PartitionSpec as P

MESH = pl.DeviceIdType.MESH
F32, BF16 = jnp.float32, jnp.bfloat16
HEADS = 16
CHUNKS = 4
BLK, D = 128, 512
COLS = 256
NBAS, OUT, OUTP = 9, 84, 96
NT = (((1,), (1,)), ((), ()))
FAR = [(0, -2), (0, -1), (1, -2), (0, 2), (1, 1), (1, 2)]

OWN, LEFT, RIGHT, UP, DOWN, UL, UR, DL, DR = range(9)
STEPS = [(0, 0), (0, -1), (0, 1), (-1, 0), (1, 0), (-1, -1), (-1, 1), (1, -1), (1, 1)]
CODE = [(r + 1) * 3 + c + 1 for r, c in STEPS]

C_UP, C_DOWN, C_AUP, C_ADOWN, C_LUP, C_LDOWN = range(6)
C_EDGE = 6
C_LON = 12
C_DIAG = C_LON + 2 * CHUNKS
N_COPIES = C_DIAG + 4 * CHUNKS


def kernel(
    n_reg, n_lon,
    nodes_h, gain_h, wqkv_h, wout_h, wlat_h, nbr_h, asg_h, psi_h, wdec_h,
    state_o, fields_o,
    xs, gain, wqkv, wout, wlat, nbr, asg, psi, psi_s, wdec, wtp,
    slots, qb, kb, vb, att, lat, edge, edges_in, onehot_e,
    hot, kron, hsel, splat, sel,
    load_sem, send_sem, recv_sem,
):
    reg, lon = lax.axis_index("reg"), lax.axis_index("lon")
    up = (lax.rem(reg + n_reg - 1, n_reg), lon)
    down = (lax.rem(reg + 1, n_reg), lon)
    left = (reg, lax.rem(lon + n_lon - 1, n_lon))
    right = (reg, lax.rem(lon + 1, n_lon))
    corners = [(v[0], h[1]) for v in (up, down) for h in (left, right)]

    barrier = pltpu.get_barrier_semaphore()
    for where in (up, down, left, right):
        pl.semaphore_signal(barrier, inc=1, device_id=where, device_id_type=MESH)

    loads = [
        pltpu.make_async_copy(src, dst, load_sem.at[k])
        for k, (src, dst) in enumerate(
            [(nodes_h, xs), (gain_h, gain), (asg_h, asg.at[1]), (psi_h, psi), (nbr_h, nbr),
             (wqkv_h, wqkv), (wdec_h, wdec), (wout_h, wout), (wlat_h, wlat), (psi_h, psi_s)]
        )
    ]
    for load in loads:
        load.start()

    def remote(k, src, dst, to):
        return pltpu.make_async_remote_copy(
            src_ref=src, dst_ref=dst, send_sem=send_sem.at[k], recv_sem=recv_sem.at[k],
            device_id=to, device_id_type=MESH,
        )

    loads[0].wait()
    loads[1].wait()
    values = xs[...].astype(F32)
    center = values - jnp.mean(values, axis=-1, keepdims=True)
    spread = jnp.mean(center * center, axis=-1, keepdims=True)
    slots[OWN] = (center * lax.rsqrt(spread + 1e-05) * gain[...]).astype(BF16)
    loads[2].wait()

    pl.semaphore_wait(barrier, 4)

    rows = BLK // CHUNKS
    copies = {}
    for c in range(CHUNKS):
        part = pl.ds(c * rows, rows)
        for side, (to, slot) in enumerate(((left, RIGHT), (right, LEFT))):
            k = C_LON + 2 * c + side
            copies[k] = remote(k, slots.at[OWN, part], slots.at[slot, part], to)
            copies[k].start()
    copies[C_UP] = remote(C_UP, slots.at[OWN], slots.at[DOWN], up)
    copies[C_DOWN] = remote(C_DOWN, slots.at[OWN], slots.at[UP], down)
    copies[C_AUP] = remote(C_AUP, asg.at[1], asg.at[2], up)
    copies[C_ADOWN] = remote(C_ADOWN, asg.at[1], asg.at[0], down)
    for k in (C_UP, C_DOWN, C_AUP, C_ADOWN):
        copies[k].start()

    def relay(c):
        part = pl.ds(c * rows, rows)
        for side, (slot, to_up, to_down) in enumerate(((RIGHT, DR, UR), (LEFT, DL, UL))):
            copies[C_LON + 2 * c + side].wait_recv()
            for v, (to, there) in enumerate(((up, to_up), (down, to_down))):
                k = C_DIAG + 4 * c + 2 * side + v
                copies[k] = remote(k, slots.at[slot, part], slots.at[there, part], to)
                copies[k].start()

    lane = lax.broadcasted_iota(jnp.int32, (8, COLS), 1)
    node = lax.broadcasted_iota(jnp.int32, (BLK, COLS), 0)

    def one_hots(blk):
        for r in range(2):
            local = jnp.broadcast_to(asg[blk, r : r + 1, :] & (BLK - 1), (8, COLS))
            for e in range(5):
                s = e - 2
                moved = pltpu.roll(local, (-s) % COLS, 1) if s else local
                if s < 0:
                    moved = jnp.where(lane < -s, -1, moved)
                if s > 0:
                    moved = jnp.where(lane >= COLS - s, -1, moved)
                tall = jnp.concatenate([moved] * (BLK // 8), axis=0)
                at = (r * 5 + e) * BLK
                hot[blk, at : at + BLK] = jnp.where(node == tall, 1.0, 0.0).astype(BF16)

    def iota(shape, dim):
        return lax.broadcasted_iota(jnp.int32, shape, dim)

    def ones_where(condition):
        return jnp.where(condition, 1.0, 0.0).astype(BF16)

    def inside(row):
        row = row + 2 * reg
        return jnp.logical_and(row >= 0, row < 2 * n_reg)

    def taps():
        return psi[...].reshape(50, NBAS).astype(BF16)

    def tap_matrices():
        spread = ones_where(iota((NBAS, NBAS * 16), 0) == iota((NBAS, NBAS * 16), 1) // 16)
        wide = jnp.dot(taps(), spread, preferred_element_type=F32).astype(BF16)
        line, tap = iota((320, 50), 0) // 16, iota((320, 50), 1)
        i, r, e = line // 10, (line // 5) % 2, line % 5
        diagonal = iota((320, NBAS * 16), 0) % 16 == iota((320, NBAS * 16), 1) % 16
        pick = ones_where(tap == ((r - i + 2) * 5 + e) * 2 + i)
        full = jnp.dot(pick, wide, preferred_element_type=F32)
        kron[...] = jnp.where(diagonal, full, 0.0).astype(BF16)

    def spread_taps():
        for n, (i, a) in enumerate(FAR):

            def at_step(e, _, n=n, i=i, a=a):
                for b in range(NBAS):
                    tap = jnp.where(inside(i + a), psi_s[a + 2, e, i, b], 0.0)
                    splat[(n * 5 + e) * NBAS + b] = jnp.full((16, 128), tap, F32).astype(BF16)
                return 0

            lax.fori_loop(0, 5, at_step, 0)

    def selections(blk):
        for i in range(2):
            taps_here = [
                (r, e, FAR.index((i, a)) * 5 + e)
                for r, a in ((r, 2 * (blk - 1) + r - i) for r in range(2))
                if (i, a) in FAR
                for e in range(5)
            ]

            def some(n, _, i=i, taps_here=taps_here):
                at = pl.multiple_of(n * 32, 32)
                hots = [hot[blk, pl.ds((r * 5 + e) * BLK + at, 32), :] for r, e, _ in taps_here]
                for b in range(NBAS):
                    total = None
                    for h, (_, _, k) in zip(hots, taps_here, strict=True):
                        tap = splat[k * NBAS + b]
                        tap = jnp.concatenate([tap, tap], axis=0)
                        tap = jnp.concatenate([tap, tap], axis=1)
                        total = tap * h if total is None else total + tap * h
                    sel[blk // 2, pl.ds(b * BLK + at, 32), pl.ds(i * COLS, COLS)] = total
                return 0

            lax.fori_loop(0, BLK // 32, some, 0)

    def halo_matrix():
        spread = ones_where(iota((NBAS * 16, NBAS), 0) // 16 == iota((NBAS * 16, NBAS), 1))
        tall = lax.dot_general(spread, taps(), NT, preferred_element_type=F32).astype(BF16)
        tap, column = iota((50, 1024), 0), iota((50, 1024), 1)
        i_t, a, e = tap % 2, tap // 10 - 2, (tap // 2) % 5 - 2
        to, cell = column // 128, column % 128
        i_out, out_col = to // 4, jnp.where(to % 4 < 2, to % 4, to % 4 + COLS - 4)
        within = cell % 16
        cell_row = jnp.where(cell < 16, 0, jnp.where(cell < 32, -2, 2)) + (within % 4) // 2
        cell_col = jnp.where(within < 4, COLS, -2) + within % 2
        real = jnp.logical_and(cell < 48, within < 8)
        match = jnp.logical_and(i_t == i_out, cell_row - i_out == a)
        match = jnp.logical_and(match, cell_col - out_col == e)
        match = jnp.logical_and(jnp.logical_and(match, real), inside(cell_row))
        every = jnp.dot(tall, ones_where(match), preferred_element_type=F32)
        line = iota((NBAS * 16, 128), 0) % 16
        mine = jnp.zeros((NBAS * 16, 128), F32)
        for to in range(8):
            mine = jnp.where(line == to, every[:, to * 128 : (to + 1) * 128], mine)
        for b in range(NBAS):
            hsel[:, b * 128 : (b + 1) * 128] = mine[b * 16 : (b + 1) * 16].astype(BF16)

    def keys_values(first, count):
        x = slots[first : first + count].reshape(count * BLK, D)
        kv = jnp.dot(x, wqkv[:, D:], preferred_element_type=F32).astype(BF16)
        for n in range(count):
            kb[CODE[first + n]] = kv[n * BLK : (n + 1) * BLK, :D]
            vb[CODE[first + n]] = kv[n * BLK : (n + 1) * BLK, D:]

    loads[3].wait()
    loads[4].wait()
    loads[9].wait()
    one_hots(1)
    tap_matrices()
    halo_matrix()
    spread_taps()
    relay(0)

    loads[5].wait()
    scale = math.log2(math.e) / math.sqrt(D // HEADS)
    projected = jnp.dot(slots[OWN], wqkv[...], preferred_element_type=F32)
    qb[...] = (projected[:, :D] * scale).astype(BF16)
    kb[CODE[OWN]] = projected[:, D : 2 * D].astype(BF16)
    vb[CODE[OWN]] = projected[:, 2 * D :].astype(BF16)

    relay(1)
    copies[C_AUP].wait_recv()
    copies[C_ADOWN].wait_recv()
    one_hots(0)
    one_hots(2)
    relay(2)
    selections(0)
    relay(3)
    keys_values(LEFT, 2)
    copies[C_UP].wait_recv()
    copies[C_DOWN].wait_recv()
    keys_values(UP, 2)
    selections(2)

    loads[6].wait()
    for o in range(OUTP // 16):
        for b in range(NBAS):
            piece = wdec[b, o * 16 : min(o * 16 + 16, OUT)]
            if piece.shape[0] < 16:
                piece = jnp.concatenate([piece, jnp.zeros((16 - piece.shape[0], D), BF16)], axis=0)
            at = (o * NBAS + b) * 16
            wtp[at : at + 16] = piece

    own = asg[1] & (BLK - 1)
    lane1 = lax.broadcasted_iota(jnp.int32, (8, 128), 1)
    marks = jnp.full((8, 128), -1, jnp.int32)
    for r in range(2):
        for side in range(2):
            piece = jnp.broadcast_to(own[r : r + 1, side * 128 : side * 128 + 128], (8, 128))
            first, source = 4 * side + 2 * r, 126 * side
            moved = pltpu.roll(piece, (first - source) % 128, 1) if first != source else piece
            marks = jnp.where(jnp.logical_and(lane1 >= first, lane1 < first + 2), moved, marks)
    tall = jnp.concatenate([marks] * (BLK // 8), axis=0)
    hits = jnp.where(node[:, :128] == tall, 1.0, 0.0)
    onehot_e[...] = jnp.transpose(hits)[:16].astype(BF16)

    for c in range(CHUNKS):
        for n in range(4):
            copies[C_DIAG + 4 * c + n].wait_recv()
    keys_values(UL, 4)

    slot = []
    for n in range(5):
        there = nbr[0, n]
        row_step = there // n_lon - reg
        col_step = lax.rem(there % n_lon - lon + 1 + n_lon, n_lon) - 1
        code = (row_step + 1) * 3 + col_step + 1
        slot.append(jnp.clip(code, 0, 8))
    head_lane = lax.broadcasted_iota(jnp.int32, (BLK, 128), 1) // 32
    ones = jnp.ones((5 * BLK, 128), BF16)
    zero = jnp.zeros((BLK, 128), BF16)
    for g in range(4):
        part = pl.ds(g * 128, 128)
        keys = jnp.concatenate([kb[s, :, part] for s in slot], axis=0)
        vals = jnp.concatenate([vb[s, :, part] for s in slot], axis=0)
        q = qb[:, part]
        wide = jnp.concatenate([jnp.where(head_lane == h, q, zero) for h in range(4)], axis=0)
        scores = lax.dot_general(wide, keys, NT, preferred_element_type=F32)
        top = jnp.max(scores, axis=-1, keepdims=True)
        weights = jnp.exp2(scores - top).astype(BF16)
        summed = jnp.dot(
            weights, jnp.concatenate([vals, ones], axis=1), preferred_element_type=F32
        )
        num, den = summed[:BLK, :128], summed[:BLK, 128:]
        for h in range(1, 4):
            mine = head_lane == h
            num = jnp.where(mine, summed[h * BLK : (h + 1) * BLK, :128], num)
            den = jnp.where(mine, summed[h * BLK : (h + 1) * BLK, 128:], den)
        att[:, part] = (num / den).astype(BF16)

    loads[7].wait()
    loads[8].wait()
    state = (
        xs[...].astype(F32) + jnp.dot(att[...], wout[...], preferred_element_type=F32)
    ).astype(BF16)
    state_o[...] = state
    v = jnp.dot(state, wlat[...], preferred_element_type=F32)
    lat[1] = (v / (1.0 + jnp.exp(-v))).astype(BF16)

    copies[C_LUP] = remote(C_LUP, lat.at[1], lat.at[2], up)
    copies[C_LDOWN] = remote(C_LDOWN, lat.at[1], lat.at[0], down)
    copies[C_LUP].start()
    copies[C_LDOWN].start()
    edge[...] = jnp.dot(onehot_e[...], lat[1], preferred_element_type=F32).astype(BF16)
    for n, (to, there) in enumerate(zip([left, right, *corners], (0, 1, 4, 5, 2, 3), strict=True)):
        copies[C_EDGE + n] = remote(C_EDGE + n, edge, edges_in.at[there], to)
        copies[C_EDGE + n].start()

    def mixed(nodes_in):
        return lax.dot_general(wtp[...], nodes_in, NT, preferred_element_type=F32).astype(BF16)

    n_out = OUTP // 16
    high = NBAS * 16

    def decode_own():
        z = mixed(lat[1])
        z = jnp.concatenate([z[o * high : (o + 1) * high] for o in range(n_out)], axis=1)
        w = jnp.dot(kron[...], z, preferred_element_type=F32).astype(BF16)
        pieces = []
        for i in range(2):
            for o in range(n_out):
                line = [w[(i * 10 + k) * 16 : (i * 10 + k + 1) * 16, o * 128 : (o + 1) * 128] for k in range(10)]
                pieces.append(jnp.concatenate(line, axis=1))
        return jnp.dot(jnp.concatenate(pieces, axis=0), hot[1], preferred_element_type=F32)

    def by_output(z):
        lines = [
            jnp.concatenate([z[o * high + b * 16 : o * high + b * 16 + 16] for b in range(NBAS)], axis=1)
            for o in range(n_out)
        ]
        return jnp.concatenate(lines, axis=0)

    def decode_far(z, k):
        return jnp.dot(by_output(z), sel[k], preferred_element_type=F32)

    total = decode_own()

    even = lax.rem(reg, 2) == 0
    near, far = jnp.where(even, 1, 0), jnp.where(even, 0, 1)
    remote(C_LUP + 1 - near, lat.at[1], lat.at[near * 2], up).wait_recv()
    other = decode_far(mixed(lat[near * 2]), near)
    remote(C_LUP + 1 - far, lat.at[1], lat.at[far * 2], up).wait_recv()
    for n in range(6):
        copies[C_EDGE + n].wait_recv()
    first4 = iota((16, D), 0) < 4
    cells = []
    for n in range(3):
        a, b = edges_in[2 * n], edges_in[2 * n + 1]
        cells.append(jnp.where(first4, a, b))
    z = mixed(jnp.concatenate([lat[far * 2]] + cells + [jnp.zeros((80, D), BF16)], axis=0))
    other += decode_far(z[:, :BLK], far)
    z = by_output(z[:, BLK:])
    sides = lax.dot_general(z, hsel[...], NT, preferred_element_type=F32)
    sides = jnp.concatenate([sides, jnp.zeros((OUTP, 112), F32)], axis=1)
    lane2 = iota((OUTP, 128), 1)
    for i in range(2):
        at_left = pltpu.roll(sides, (-4 * i) % 128, 1) if i else sides
        at_left = jnp.where(lane2 < 2, at_left, 0.0)
        at_right = jnp.where(lane2 >= 126, pltpu.roll(sides, 124 - 4 * i, 1), 0.0)
        whole = total[i * OUTP : (i + 1) * OUTP] + other[:, i * COLS : (i + 1) * COLS]
        whole += jnp.concatenate([at_left, at_right], axis=1)
        fields_o[i] = whole[:OUT].astype(BF16)

    for copy in copies.values():
        copy.wait_send()


def shards(sizes, nodes, norm_gain, w_qkv, w_out, w_latent, neighbours, assignment, psi, w_dec):
    anywhere = pl.BlockSpec(memory_space=pl.ANY)
    vmem = pl.BlockSpec(memory_space=pltpu.VMEM)
    state, fields = pl.pallas_call(
        functools.partial(kernel, *sizes),
        out_shape=(
            pltpu.VMEM((BLK, D), BF16),
            pltpu.VMEM((2, OUT, COLS), BF16),
        ),
        in_specs=[anywhere] * 9,
        out_specs=(vmem, vmem),
        scratch_shapes=[
            pltpu.VMEM((BLK, D), BF16),
            pltpu.VMEM((1, D), F32),
            pltpu.VMEM((D, 3 * D), BF16),
            pltpu.VMEM((D, D), BF16),
            pltpu.VMEM((D, D), BF16),
            pltpu.SMEM((1, 5), jnp.int32),
            pltpu.VMEM((3, 2, COLS), jnp.int32),
            pltpu.VMEM((5, 5, 2, NBAS), F32),
            pltpu.SMEM((5, 5, 2, NBAS), F32),
            pltpu.VMEM((NBAS, OUT, D), BF16),
            pltpu.VMEM((NBAS * OUTP, D), BF16),
            pltpu.VMEM((9, BLK, D), BF16),
            pltpu.VMEM((BLK, D), BF16),
            pltpu.VMEM((9, BLK, D), BF16),
            pltpu.VMEM((9, BLK, D), BF16),
            pltpu.VMEM((BLK, D), BF16),
            pltpu.VMEM((3, BLK, D), BF16),
            pltpu.VMEM((16, D), BF16),
            pltpu.VMEM((6, 16, D), BF16),
            pltpu.VMEM((16, 128), BF16),
            pltpu.VMEM((3, 10 * BLK, COLS), BF16),
            pltpu.VMEM((320, NBAS * 16), BF16),
            pltpu.VMEM((16, NBAS * 128), BF16),
            pltpu.VMEM((30 * NBAS, 16, 128), BF16),
            pltpu.VMEM((2, NBAS * BLK, 2 * COLS), BF16),
            pltpu.SemaphoreType.DMA((10,)),
            pltpu.SemaphoreType.DMA((N_COPIES,)),
            pltpu.SemaphoreType.DMA((N_COPIES,)),
        ],
        compiler_params=pltpu.CompilerParams(
            collective_id=0, has_side_effects=True, vmem_limit_bytes=56 * 2**20
        ),
    )(
        nodes[0], norm_gain[None], w_qkv, w_out, w_latent, neighbours, assignment,
        psi.transpose(2, 3, 1, 0), w_dec.transpose(0, 2, 1),
    )
    return state[None], fields.transpose(1, 0, 2)[None]


def solution(mesh):
    sizes = (mesh.shape["reg"], mesh.shape["lon"])
    in_specs = (
        P(None, ("reg", "lon"), None),
        P(),
        P(),
        P(),
        P(),
        P(("reg", "lon"), None),
        P("reg", "lon"),
        P(None, "reg", None, None),
        P(),
    )
    out_specs = (P(None, ("reg", "lon"), None), P(None, None, "reg", "lon"))
    return jax.shard_map(
        functools.partial(shards, sizes),
        mesh=mesh,
        in_specs=in_specs,
        out_specs=out_specs,
        check_vma=False,
    )
```

```python
import functools
import math

import jax
import jax.numpy as jnp
from jax import lax
from jax.experimental import pallas as pl
from jax.experimental.pallas import tpu as pltpu
from jax.sharding import PartitionSpec as P

MESH = pl.DeviceIdType.MESH
F32, BF16 = jnp.float32, jnp.bfloat16
HEADS = 16
CHUNKS = 4
BLK, D = 128, 512
COLS = 256
NBAS, OUT, OUTP = 9, 84, 96
NT = (((1,), (1,)), ((), ()))
FAR = [(0, -2), (0, -1), (1, -2), (0, 2), (1, 1), (1, 2)]

OWN, LEFT, RIGHT, UP, DOWN, UL, UR, DL, DR = range(9)
STEPS = [(0, 0), (0, -1), (0, 1), (-1, 0), (1, 0), (-1, -1), (-1, 1), (1, -1), (1, 1)]
CODE = [(r + 1) * 3 + c + 1 for r, c in STEPS]

C_UP, C_DOWN, C_AUP, C_ADOWN, C_LUP, C_LDOWN = range(6)
C_EDGE = 6
C_LON = 12
C_DIAG = C_LON + 2 * CHUNKS
N_COPIES = C_DIAG + 4 * CHUNKS


def kernel(
    n_reg, n_lon,
    nodes_h, gain_h, wqkv_h, wout_h, wlat_h, nbr_h, asg_h, psi_h, wdec_h,
    state_o, fields_o,
    xs, gain, wqkv, wout, wlat, nbr, asg, psi, psi_s, wdec, wtp,
    slots, qb, kb, vb, att, lat, edge, edges_in, onehot_e,
    hot, kron, hsel, splat, sel,
    load_sem, send_sem, recv_sem,
):
    reg, lon = lax.axis_index("reg"), lax.axis_index("lon")
    up = (lax.rem(reg + n_reg - 1, n_reg), lon)
    down = (lax.rem(reg + 1, n_reg), lon)
    left = (reg, lax.rem(lon + n_lon - 1, n_lon))
    right = (reg, lax.rem(lon + 1, n_lon))
    corners = [(v[0], h[1]) for v in (up, down) for h in (left, right)]

    has_up, has_down = reg > 0, reg < n_reg - 1

    barrier = pltpu.get_barrier_semaphore()

    def greet(where):
        pl.semaphore_signal(barrier, inc=1, device_id=where, device_id_type=MESH)

    greet(left)
    greet(right)
    pl.when(has_up)(lambda: greet(up))
    pl.when(has_down)(lambda: greet(down))

    loads = [
        pltpu.make_async_copy(src, dst, load_sem.at[k])
        for k, (src, dst) in enumerate(
            [(nodes_h, xs), (gain_h, gain), (asg_h, asg.at[1]), (psi_h, psi), (nbr_h, nbr),
             (wqkv_h, wqkv), (wdec_h, wdec), (wout_h, wout), (wlat_h, wlat), (psi_h, psi_s)]
        )
    ]
    for load in loads:
        load.start()

    def remote(k, src, dst, to):
        return pltpu.make_async_remote_copy(
            src_ref=src, dst_ref=dst, send_sem=send_sem.at[k], recv_sem=recv_sem.at[k],
            device_id=to, device_id_type=MESH,
        )

    loads[0].wait()
    loads[1].wait()
    values = xs[...].astype(F32)
    center = values - jnp.mean(values, axis=-1, keepdims=True)
    spread = jnp.mean(center * center, axis=-1, keepdims=True)
    slots[OWN] = (center * lax.rsqrt(spread + 1e-05) * gain[...]).astype(BF16)
    loads[2].wait()

    pl.semaphore_wait(barrier, 2 + has_up.astype(jnp.int32) + has_down.astype(jnp.int32))

    rows = BLK // CHUNKS
    copies = {}
    for c in range(CHUNKS):
        part = pl.ds(c * rows, rows)
        for side, (to, slot) in enumerate(((left, RIGHT), (right, LEFT))):
            k = C_LON + 2 * c + side
            copies[k] = remote(k, slots.at[OWN, part], slots.at[slot, part], to)
            copies[k].start()
    copies[C_UP] = remote(C_UP, slots.at[OWN], slots.at[DOWN], up)
    copies[C_DOWN] = remote(C_DOWN, slots.at[OWN], slots.at[UP], down)
    copies[C_AUP] = remote(C_AUP, asg.at[1], asg.at[2], up)
    copies[C_ADOWN] = remote(C_ADOWN, asg.at[1], asg.at[0], down)

    upward, downward = [C_UP, C_AUP], [C_DOWN, C_ADOWN]

    def start_all(keys):
        for k in keys:
            copies[k].start()

    def wait_all(keys):
        for k in keys:
            copies[k].wait_recv()

    pl.when(has_up)(lambda: start_all([C_UP, C_AUP]))
    pl.when(has_down)(lambda: start_all([C_DOWN, C_ADOWN]))

    def clear(blk):
        lat[blk] = jnp.zeros((BLK, D), BF16)
        asg[blk] = jnp.zeros((2, COLS), jnp.int32)
        for n in (0, 1):
            edges_in[blk + 2 + n] = jnp.zeros((16, D), BF16)
        for slot in (UP, UL, UR) if blk == 0 else (DOWN, DL, DR):
            slots[slot] = jnp.zeros((BLK, D), BF16)

    pl.when(jnp.logical_not(has_up))(lambda: clear(0))
    pl.when(jnp.logical_not(has_down))(lambda: clear(2))

    def relay(c):
        part = pl.ds(c * rows, rows)
        for side, (slot, to_up, to_down) in enumerate(((RIGHT, DR, UR), (LEFT, DL, UL))):
            copies[C_LON + 2 * c + side].wait_recv()
            for v, (to, there) in enumerate(((up, to_up), (down, to_down))):
                k = C_DIAG + 4 * c + 2 * side + v
                copies[k] = remote(k, slots.at[slot, part], slots.at[there, part], to)
        ups, downs = ([C_DIAG + 4 * c + 2 * side + v for side in (0, 1)] for v in (0, 1))
        upward.extend(ups)
        downward.extend(downs)
        pl.when(has_up)(lambda: start_all(ups))
        pl.when(has_down)(lambda: start_all(downs))

    lane = lax.broadcasted_iota(jnp.int32, (8, COLS), 1)
    node = lax.broadcasted_iota(jnp.int32, (BLK, COLS), 0)

    def one_hots(blk):
        for r in range(2):
            local = jnp.broadcast_to(asg[blk, r : r + 1, :] & (BLK - 1), (8, COLS))
            for e in range(5):
                s = e - 2
                moved = pltpu.roll(local, (-s) % COLS, 1) if s else local
                if s < 0:
                    moved = jnp.where(lane < -s, -1, moved)
                if s > 0:
                    moved = jnp.where(lane >= COLS - s, -1, moved)
                tall = jnp.concatenate([moved] * (BLK // 8), axis=0)
                at = (r * 5 + e) * BLK
                hot[blk, at : at + BLK] = jnp.where(node == tall, 1.0, 0.0).astype(BF16)

    def iota(shape, dim):
        return lax.broadcasted_iota(jnp.int32, shape, dim)

    def ones_where(condition):
        return jnp.where(condition, 1.0, 0.0).astype(BF16)

    def inside(row):
        row = row + 2 * reg
        return jnp.logical_and(row >= 0, row < 2 * n_reg)

    def taps():
        return psi[...].reshape(50, NBAS).astype(BF16)

    def tap_matrices():
        spread = ones_where(iota((NBAS, NBAS * 16), 0) == iota((NBAS, NBAS * 16), 1) // 16)
        wide = jnp.dot(taps(), spread, preferred_element_type=F32).astype(BF16)
        line, tap = iota((320, 50), 0) // 16, iota((320, 50), 1)
        i, r, e = line // 10, (line // 5) % 2, line % 5
        diagonal = iota((320, NBAS * 16), 0) % 16 == iota((320, NBAS * 16), 1) % 16
        pick = ones_where(tap == ((r - i + 2) * 5 + e) * 2 + i)
        full = jnp.dot(pick, wide, preferred_element_type=F32)
        kron[...] = jnp.where(diagonal, full, 0.0).astype(BF16)

    def spread_taps():
        for n, (i, a) in enumerate(FAR):

            def at_step(e, _, n=n, i=i, a=a):
                for b in range(NBAS):
                    tap = jnp.where(inside(i + a), psi_s[a + 2, e, i, b], 0.0)
                    splat[(n * 5 + e) * NBAS + b] = jnp.full((16, 128), tap, F32).astype(BF16)
                return 0

            lax.fori_loop(0, 5, at_step, 0)

    def selections(blk):
        for i in range(2):
            taps_here = [
                (r, e, FAR.index((i, a)) * 5 + e)
                for r, a in ((r, 2 * (blk - 1) + r - i) for r in range(2))
                if (i, a) in FAR
                for e in range(5)
            ]

            def some(n, _, i=i, taps_here=taps_here):
                at = pl.multiple_of(n * 32, 32)
                hots = [hot[blk, pl.ds((r * 5 + e) * BLK + at, 32), :] for r, e, _ in taps_here]
                for b in range(NBAS):
                    total = None
                    for h, (_, _, k) in zip(hots, taps_here, strict=True):
                        tap = splat[k * NBAS + b]
                        tap = jnp.concatenate([tap, tap], axis=0)
                        tap = jnp.concatenate([tap, tap], axis=1)
                        total = tap * h if total is None else total + tap * h
                    sel[blk // 2, pl.ds(b * BLK + at, 32), pl.ds(i * COLS, COLS)] = total
                return 0

            lax.fori_loop(0, BLK // 32, some, 0)

    def halo_matrix():
        spread = ones_where(iota((NBAS * 16, NBAS), 0) // 16 == iota((NBAS * 16, NBAS), 1))
        tall = lax.dot_general(spread, taps(), NT, preferred_element_type=F32).astype(BF16)
        tap, column = iota((50, 1024), 0), iota((50, 1024), 1)
        i_t, a, e = tap % 2, tap // 10 - 2, (tap // 2) % 5 - 2
        to, cell = column // 128, column % 128
        i_out, out_col = to // 4, jnp.where(to % 4 < 2, to % 4, to % 4 + COLS - 4)
        within = cell % 16
        cell_row = jnp.where(cell < 16, 0, jnp.where(cell < 32, -2, 2)) + (within % 4) // 2
        cell_col = jnp.where(within < 4, COLS, -2) + within % 2
        real = jnp.logical_and(cell < 48, within < 8)
        match = jnp.logical_and(i_t == i_out, cell_row - i_out == a)
        match = jnp.logical_and(match, cell_col - out_col == e)
        match = jnp.logical_and(jnp.logical_and(match, real), inside(cell_row))
        every = jnp.dot(tall, ones_where(match), preferred_element_type=F32)
        line = iota((NBAS * 16, 128), 0) % 16
        mine = jnp.zeros((NBAS * 16, 128), F32)
        for to in range(8):
            mine = jnp.where(line == to, every[:, to * 128 : (to + 1) * 128], mine)
        for b in range(NBAS):
            hsel[:, b * 128 : (b + 1) * 128] = mine[b * 16 : (b + 1) * 16].astype(BF16)

    def keys_values(first, count, start=0, height=BLK):
        part = pl.ds(start, height)
        x = jnp.concatenate([slots[first + n, part] for n in range(count)], axis=0)
        kv = jnp.dot(x, wqkv[:, D:], preferred_element_type=F32).astype(BF16)
        for n in range(count):
            kb[CODE[first + n], part] = kv[n * height : (n + 1) * height, :D]
            vb[CODE[first + n], part] = kv[n * height : (n + 1) * height, D:]

    loads[3].wait()
    loads[4].wait()
    loads[9].wait()
    one_hots(1)
    tap_matrices()
    halo_matrix()
    spread_taps()
    relay(0)

    loads[5].wait()
    scale = math.log2(math.e) / math.sqrt(D // HEADS)
    projected = jnp.dot(slots[OWN], wqkv[...], preferred_element_type=F32)
    qb[...] = (projected[:, :D] * scale).astype(BF16)
    kb[CODE[OWN]] = projected[:, D : 2 * D].astype(BF16)
    vb[CODE[OWN]] = projected[:, 2 * D :].astype(BF16)

    relay(1)
    pl.when(has_down)(lambda: wait_all([C_AUP]))
    pl.when(has_up)(lambda: wait_all([C_ADOWN]))
    one_hots(0)
    one_hots(2)
    relay(2)
    selections(0)
    relay(3)
    keys_values(LEFT, 2)
    pl.when(has_down)(lambda: wait_all([C_UP]))
    pl.when(has_up)(lambda: wait_all([C_DOWN]))
    keys_values(UP, 2)
    selections(2)

    loads[6].wait()
    for o in range(OUTP // 16):
        for b in range(NBAS):
            piece = wdec[b, o * 16 : min(o * 16 + 16, OUT)]
            if piece.shape[0] < 16:
                piece = jnp.concatenate([piece, jnp.zeros((16 - piece.shape[0], D), BF16)], axis=0)
            at = (o * NBAS + b) * 16
            wtp[at : at + 16] = piece

    own = asg[1] & (BLK - 1)
    lane1 = lax.broadcasted_iota(jnp.int32, (8, 128), 1)
    marks = jnp.full((8, 128), -1, jnp.int32)
    for r in range(2):
        for side in range(2):
            piece = jnp.broadcast_to(own[r : r + 1, side * 128 : side * 128 + 128], (8, 128))
            first, source = 4 * side + 2 * r, 126 * side
            moved = pltpu.roll(piece, (first - source) % 128, 1) if first != source else piece
            marks = jnp.where(jnp.logical_and(lane1 >= first, lane1 < first + 2), moved, marks)
    tall = jnp.concatenate([marks] * (BLK // 8), axis=0)
    hits = jnp.where(node[:, :128] == tall, 1.0, 0.0)
    onehot_e[...] = jnp.transpose(hits)[:16].astype(BF16)

    for half in range(2):
        chunks = range(half * CHUNKS // 2, (half + 1) * CHUNKS // 2)
        from_down, from_up = (
            [C_DIAG + 4 * c + 2 * side + v for c in chunks for side in (0, 1)] for v in (0, 1)
        )
        pl.when(has_down)(lambda keys=from_down: wait_all(keys))
        pl.when(has_up)(lambda keys=from_up: wait_all(keys))
        keys_values(UL, 4, half * (BLK // 2), BLK // 2)

    slot = []
    for n in range(5):
        there = nbr[0, n]
        row_step = there // n_lon - reg
        col_step = lax.rem(there % n_lon - lon + 1 + n_lon, n_lon) - 1
        code = (row_step + 1) * 3 + col_step + 1
        slot.append(jnp.clip(code, 0, 8))
    head_lane = lax.broadcasted_iota(jnp.int32, (BLK, 128), 1) // 32
    ones = jnp.ones((5 * BLK, 128), BF16)
    zero = jnp.zeros((BLK, 128), BF16)
    for g in range(4):
        part = pl.ds(g * 128, 128)
        keys = jnp.concatenate([kb[s, :, part] for s in slot], axis=0)
        vals = jnp.concatenate([vb[s, :, part] for s in slot], axis=0)
        q = qb[:, part]
        wide = jnp.concatenate([jnp.where(head_lane == h, q, zero) for h in range(4)], axis=0)
        scores = lax.dot_general(wide, keys, NT, preferred_element_type=F32)
        top = jnp.max(scores, axis=-1, keepdims=True)
        weights = jnp.exp2(scores - top).astype(BF16)
        summed = jnp.dot(
            weights, jnp.concatenate([vals, ones], axis=1), preferred_element_type=F32
        )
        num, den = summed[:BLK, :128], summed[:BLK, 128:]
        for h in range(1, 4):
            mine = head_lane == h
            num = jnp.where(mine, summed[h * BLK : (h + 1) * BLK, :128], num)
            den = jnp.where(mine, summed[h * BLK : (h + 1) * BLK, 128:], den)
        att[:, part] = (num / den).astype(BF16)

    loads[7].wait()
    loads[8].wait()
    state = (
        xs[...].astype(F32) + jnp.dot(att[...], wout[...], preferred_element_type=F32)
    ).astype(BF16)
    state_o[...] = state
    v = jnp.dot(state, wlat[...], preferred_element_type=F32)
    lat[1] = (v / (1.0 + jnp.exp(-v))).astype(BF16)

    edge[...] = jnp.dot(onehot_e[...], lat[1], preferred_element_type=F32).astype(BF16)
    for n, (to, there) in enumerate(zip([left, right, *corners], (0, 1, 4, 5, 2, 3), strict=True)):
        copies[C_EDGE + n] = remote(C_EDGE + n, edge, edges_in.at[there], to)
    copies[C_LUP] = remote(C_LUP, lat.at[1], lat.at[2], up)
    copies[C_LDOWN] = remote(C_LDOWN, lat.at[1], lat.at[0], down)
    start_all([C_EDGE, C_EDGE + 1])
    pl.when(has_up)(lambda: start_all([C_EDGE + 2, C_EDGE + 3, C_LUP]))
    pl.when(has_down)(lambda: start_all([C_EDGE + 4, C_EDGE + 5, C_LDOWN]))
    upward.extend([C_EDGE + 2, C_EDGE + 3, C_LUP])
    downward.extend([C_EDGE + 4, C_EDGE + 5, C_LDOWN])

    def mixed(nodes_in):
        return lax.dot_general(wtp[...], nodes_in, NT, preferred_element_type=F32).astype(BF16)

    n_out = OUTP // 16
    high = NBAS * 16

    def decode_own():
        z = mixed(lat[1])
        z = jnp.concatenate([z[o * high : (o + 1) * high] for o in range(n_out)], axis=1)
        w = jnp.dot(kron[...], z, preferred_element_type=F32).astype(BF16)
        pieces = []
        for i in range(2):
            for o in range(n_out):
                line = [w[(i * 10 + k) * 16 : (i * 10 + k + 1) * 16, o * 128 : (o + 1) * 128] for k in range(10)]
                pieces.append(jnp.concatenate(line, axis=1))
        return jnp.dot(jnp.concatenate(pieces, axis=0), hot[1], preferred_element_type=F32)

    def by_output(z):
        lines = [
            jnp.concatenate([z[o * high + b * 16 : o * high + b * 16 + 16] for b in range(NBAS)], axis=1)
            for o in range(n_out)
        ]
        return jnp.concatenate(lines, axis=0)

    def decode_far(z, k):
        return jnp.dot(by_output(z), sel[k], preferred_element_type=F32)

    total = decode_own()

    even = lax.rem(reg, 2) == 0
    near, far = jnp.where(even, 1, 0), jnp.where(even, 0, 1)
    remote(C_LUP + 1 - near, lat.at[1], lat.at[near * 2], up).wait_recv()
    other = decode_far(mixed(lat[near * 2]), near)
    has_far = jnp.logical_or(jnp.logical_and(even, has_up), jnp.logical_and(reg % 2 == 1, has_down))

    @pl.when(has_far)
    def _():
        remote(C_LUP + 1 - far, lat.at[1], lat.at[far * 2], up).wait_recv()

    wait_all([C_EDGE, C_EDGE + 1])
    pl.when(has_down)(lambda: wait_all([C_EDGE + 2, C_EDGE + 3]))
    pl.when(has_up)(lambda: wait_all([C_EDGE + 4, C_EDGE + 5]))
    first4 = iota((16, D), 0) < 4
    cells = []
    for n in range(3):
        a, b = edges_in[2 * n], edges_in[2 * n + 1]
        cells.append(jnp.where(first4, a, b))
    z = mixed(jnp.concatenate([lat[far * 2]] + cells + [jnp.zeros((80, D), BF16)], axis=0))
    other += decode_far(z[:, :BLK], far)
    z = by_output(z[:, BLK:])
    sides = lax.dot_general(z, hsel[...], NT, preferred_element_type=F32)
    sides = jnp.concatenate([sides, jnp.zeros((OUTP, 112), F32)], axis=1)
    lane2 = iota((OUTP, 128), 1)
    for i in range(2):
        at_left = pltpu.roll(sides, (-4 * i) % 128, 1) if i else sides
        at_left = jnp.where(lane2 < 2, at_left, 0.0)
        at_right = jnp.where(lane2 >= 126, pltpu.roll(sides, 124 - 4 * i, 1), 0.0)
        whole = total[i * OUTP : (i + 1) * OUTP] + other[:, i * COLS : (i + 1) * COLS]
        whole += jnp.concatenate([at_left, at_right], axis=1)
        fields_o[:, i, :] = whole[:OUT].astype(BF16)

    def sent(keys):
        for k in keys:
            copies[k].wait_send()

    sent([k for k in copies if k not in upward and k not in downward])
    pl.when(has_up)(lambda: sent(upward))
    pl.when(has_down)(lambda: sent(downward))


def store(state, fields, state_o, fields_o, sem):
    copies = [
        pltpu.make_async_copy(state, state_o, sem.at[0]),
        pltpu.make_async_copy(fields, fields_o, sem.at[1]),
    ]
    for copy in copies:
        copy.start()
    for copy in copies:
        copy.wait()


def shards(sizes, nodes, norm_gain, w_qkv, w_out, w_latent, neighbours, assignment, psi, w_dec):
    anywhere = pl.BlockSpec(memory_space=pl.ANY)
    vmem = pl.BlockSpec(memory_space=pltpu.VMEM)
    state, fields = pl.pallas_call(
        functools.partial(kernel, *sizes),
        out_shape=(
            pltpu.VMEM((BLK, D), BF16),
            pltpu.VMEM((OUT, 2, COLS), BF16),
        ),
        in_specs=[anywhere] * 9,
        out_specs=(vmem, vmem),
        scratch_shapes=[
            pltpu.VMEM((BLK, D), BF16),
            pltpu.VMEM((1, D), F32),
            pltpu.VMEM((D, 3 * D), BF16),
            pltpu.VMEM((D, D), BF16),
            pltpu.VMEM((D, D), BF16),
            pltpu.SMEM((1, 5), jnp.int32),
            pltpu.VMEM((3, 2, COLS), jnp.int32),
            pltpu.VMEM((5, 5, 2, NBAS), F32),
            pltpu.SMEM((5, 5, 2, NBAS), F32),
            pltpu.VMEM((NBAS, OUT, D), BF16),
            pltpu.VMEM((NBAS * OUTP, D), BF16),
            pltpu.VMEM((9, BLK, D), BF16),
            pltpu.VMEM((BLK, D), BF16),
            pltpu.VMEM((9, BLK, D), BF16),
            pltpu.VMEM((9, BLK, D), BF16),
            pltpu.VMEM((BLK, D), BF16),
            pltpu.VMEM((3, BLK, D), BF16),
            pltpu.VMEM((16, D), BF16),
            pltpu.VMEM((6, 16, D), BF16),
            pltpu.VMEM((16, 128), BF16),
            pltpu.VMEM((3, 10 * BLK, COLS), BF16),
            pltpu.VMEM((320, NBAS * 16), BF16),
            pltpu.VMEM((16, NBAS * 128), BF16),
            pltpu.VMEM((30 * NBAS, 16, 128), BF16),
            pltpu.VMEM((2, NBAS * BLK, 2 * COLS), BF16),
            pltpu.SemaphoreType.DMA((10,)),
            pltpu.SemaphoreType.DMA((N_COPIES,)),
            pltpu.SemaphoreType.DMA((N_COPIES,)),
        ],
        compiler_params=pltpu.CompilerParams(
            collective_id=0, has_side_effects=True, vmem_limit_bytes=56 * 2**20
        ),
    )(
        nodes[0], norm_gain[None], w_qkv, w_out, w_latent, neighbours, assignment,
        psi.transpose(2, 3, 1, 0), w_dec.transpose(0, 2, 1),
    )
    state, fields = pl.pallas_call(
        store,
        out_shape=(
            jax.ShapeDtypeStruct((BLK, D), BF16),
            jax.ShapeDtypeStruct((OUT, 2, COLS), BF16),
        ),
        in_specs=[vmem] * 2,
        out_specs=(anywhere, anywhere),
        scratch_shapes=[pltpu.SemaphoreType.DMA((2,))],
    )(
        pltpu.with_memory_space_constraint(state, pltpu.VMEM),
        pltpu.with_memory_space_constraint(fields, pltpu.VMEM),
    )
    return state[None], fields[None]


def solution(mesh):
    sizes = (mesh.shape["reg"], mesh.shape["lon"])
    in_specs = (
        P(None, ("reg", "lon"), None),
        P(),
        P(),
        P(),
        P(),
        P(("reg", "lon"), None),
        P("reg", "lon"),
        P(None, "reg", None, None),
        P(),
    )
    out_specs = (P(None, ("reg", "lon"), None), P(None, None, "reg", "lon"))
    return jax.shard_map(
        functools.partial(shards, sizes),
        mesh=mesh,
        in_specs=in_specs,
        out_specs=out_specs,
        check_vma=False,
    )
```

```python
import functools
import math

import jax
import jax.numpy as jnp
from jax import lax
from jax.experimental import pallas as pl
from jax.experimental.pallas import tpu as pltpu
from jax.sharding import PartitionSpec as P

MESH = pl.DeviceIdType.MESH
F32, BF16 = jnp.float32, jnp.bfloat16
HEADS = 16
CHUNKS = 4
BLK, D = 128, 512
COLS = 256
NBAS, OUT, OUTP = 9, 84, 96
NT = (((1,), (1,)), ((), ()))
FAR = [(0, -2), (0, -1), (1, -2), (0, 2), (1, 1), (1, 2)]

OWN, LEFT, RIGHT, UP, DOWN, UL, UR, DL, DR = range(9)
STEPS = [(0, 0), (0, -1), (0, 1), (-1, 0), (1, 0), (-1, -1), (-1, 1), (1, -1), (1, 1)]
CODE = [(r + 1) * 3 + c + 1 for r, c in STEPS]

C_UP, C_DOWN, C_AUP, C_ADOWN, C_LUP, C_LDOWN = range(6)
C_EDGE = 6
C_LON = 12
C_DIAG = C_LON + 2 * CHUNKS
N_COPIES = C_DIAG + 4 * CHUNKS


def kernel(
    n_reg, n_lon,
    nodes_h, gain_h, wqkv_h, wout_h, wlat_h, nbr_h, asg_h, psi_h, wdec_h,
    state_o, fields_o,
    xs, gain, wqkv, wout, wlat, nbr, asg, psi, psi_s, wdec, wtp,
    slots, qb, kb, vb, own_num, own_den, own_top, att, lat, edge, edges_in, onehot_e,
    hot, kron, hsel, splat, sel, other,
    load_sem, send_sem, recv_sem,
):
    reg, lon = lax.axis_index("reg"), lax.axis_index("lon")
    up = (lax.rem(reg + n_reg - 1, n_reg), lon)
    down = (lax.rem(reg + 1, n_reg), lon)
    left = (reg, lax.rem(lon + n_lon - 1, n_lon))
    right = (reg, lax.rem(lon + 1, n_lon))
    corners = [(v[0], h[1]) for v in (up, down) for h in (left, right)]

    has_up, has_down = reg > 0, reg < n_reg - 1

    barrier = pltpu.get_barrier_semaphore()

    def greet(where):
        pl.semaphore_signal(barrier, inc=1, device_id=where, device_id_type=MESH)

    greet(left)
    greet(right)
    pl.when(has_up)(lambda: greet(up))
    pl.when(has_down)(lambda: greet(down))

    loads = [
        pltpu.make_async_copy(src, dst, load_sem.at[k])
        for k, (src, dst) in enumerate(
            [(nodes_h, xs), (gain_h, gain), (asg_h, asg.at[1]), (psi_h, psi), (nbr_h, nbr),
             (wqkv_h, wqkv), (wdec_h, wdec), (wout_h, wout), (wlat_h, wlat), (psi_h, psi_s)]
        )
    ]
    for load in loads:
        load.start()

    def remote(k, src, dst, to):
        return pltpu.make_async_remote_copy(
            src_ref=src, dst_ref=dst, send_sem=send_sem.at[k], recv_sem=recv_sem.at[k],
            device_id=to, device_id_type=MESH,
        )

    loads[0].wait()
    loads[1].wait()
    values = xs[...].astype(F32)
    center = values - jnp.mean(values, axis=-1, keepdims=True)
    spread = jnp.mean(center * center, axis=-1, keepdims=True)
    slots[OWN] = (center * lax.rsqrt(spread + 1e-05) * gain[...]).astype(BF16)
    loads[2].wait()

    pl.semaphore_wait(barrier, 2 + has_up.astype(jnp.int32) + has_down.astype(jnp.int32))

    rows = BLK // CHUNKS
    copies = {}
    for c in range(CHUNKS):
        part = pl.ds(c * rows, rows)
        for side, (to, slot) in enumerate(((left, RIGHT), (right, LEFT))):
            k = C_LON + 2 * c + side
            copies[k] = remote(k, slots.at[OWN, part], slots.at[slot, part], to)
            copies[k].start()
    copies[C_UP] = remote(C_UP, slots.at[OWN], slots.at[DOWN], up)
    copies[C_DOWN] = remote(C_DOWN, slots.at[OWN], slots.at[UP], down)
    copies[C_AUP] = remote(C_AUP, asg.at[1], asg.at[2], up)
    copies[C_ADOWN] = remote(C_ADOWN, asg.at[1], asg.at[0], down)

    upward, downward = [C_UP, C_AUP], [C_DOWN, C_ADOWN]

    def start_all(keys):
        for k in keys:
            copies[k].start()

    def wait_all(keys):
        for k in keys:
            copies[k].wait_recv()

    pl.when(has_up)(lambda: start_all([C_UP, C_AUP]))
    pl.when(has_down)(lambda: start_all([C_DOWN, C_ADOWN]))

    def clear(blk):
        lat[blk] = jnp.zeros((BLK, D), BF16)
        asg[blk] = jnp.zeros((2, COLS), jnp.int32)
        for n in (0, 1):
            edges_in[blk + 2 + n] = jnp.zeros((16, D), BF16)
        for slot in (UP, UL, UR) if blk == 0 else (DOWN, DL, DR):
            slots[slot] = jnp.zeros((BLK, D), BF16)

    pl.when(jnp.logical_not(has_up))(lambda: clear(0))
    pl.when(jnp.logical_not(has_down))(lambda: clear(2))

    def relay(c):
        part = pl.ds(c * rows, rows)
        for side, (slot, to_up, to_down) in enumerate(((RIGHT, DR, UR), (LEFT, DL, UL))):
            copies[C_LON + 2 * c + side].wait_recv()
            for v, (to, there) in enumerate(((up, to_up), (down, to_down))):
                k = C_DIAG + 4 * c + 2 * side + v
                copies[k] = remote(k, slots.at[slot, part], slots.at[there, part], to)
        ups, downs = ([C_DIAG + 4 * c + 2 * side + v for side in (0, 1)] for v in (0, 1))
        upward.extend(ups)
        downward.extend(downs)
        pl.when(has_up)(lambda: start_all(ups))
        pl.when(has_down)(lambda: start_all(downs))

    lane = lax.broadcasted_iota(jnp.int32, (8, COLS), 1)
    node = lax.broadcasted_iota(jnp.int32, (BLK, COLS), 0)

    def one_hots(blk):
        for r in range(2):
            local = jnp.broadcast_to(asg[blk, r : r + 1, :] & (BLK - 1), (8, COLS))
            for e in range(5):
                s = e - 2
                moved = pltpu.roll(local, (-s) % COLS, 1) if s else local
                if s < 0:
                    moved = jnp.where(lane < -s, -1, moved)
                if s > 0:
                    moved = jnp.where(lane >= COLS - s, -1, moved)
                tall = jnp.concatenate([moved] * (BLK // 8), axis=0)
                at = (r * 5 + e) * BLK
                hot[blk, at : at + BLK] = jnp.where(node == tall, 1.0, 0.0).astype(BF16)

    def iota(shape, dim):
        return lax.broadcasted_iota(jnp.int32, shape, dim)

    def ones_where(condition):
        return jnp.where(condition, 1.0, 0.0).astype(BF16)

    def inside(row):
        row = row + 2 * reg
        return jnp.logical_and(row >= 0, row < 2 * n_reg)

    def taps():
        return psi[...].reshape(50, NBAS).astype(BF16)

    def tap_matrices():
        spread = ones_where(iota((NBAS, NBAS * 16), 0) == iota((NBAS, NBAS * 16), 1) // 16)
        wide = jnp.dot(taps(), spread, preferred_element_type=F32).astype(BF16)
        line, tap = iota((320, 50), 0) // 16, iota((320, 50), 1)
        i, r, e = line // 10, (line // 5) % 2, line % 5
        diagonal = iota((320, NBAS * 16), 0) % 16 == iota((320, NBAS * 16), 1) % 16
        pick = ones_where(tap == ((r - i + 2) * 5 + e) * 2 + i)
        full = jnp.dot(pick, wide, preferred_element_type=F32)
        kron[...] = jnp.where(diagonal, full, 0.0).astype(BF16)

    def spread_taps():
        for n, (i, a) in enumerate(FAR):

            def at_step(e, _, n=n, i=i, a=a):
                for b in range(NBAS):
                    tap = jnp.where(inside(i + a), psi_s[a + 2, e, i, b], 0.0)
                    splat[(n * 5 + e) * NBAS + b] = jnp.full((16, 128), tap, F32).astype(BF16)
                return 0

            lax.fori_loop(0, 5, at_step, 0)

    def selections(blk):
        for i in range(2):
            taps_here = [
                (r, e, FAR.index((i, a)) * 5 + e)
                for r, a in ((r, 2 * (blk - 1) + r - i) for r in range(2))
                if (i, a) in FAR
                for e in range(5)
            ]

            def some(n, _, i=i, taps_here=taps_here):
                at = pl.multiple_of(n * 32, 32)
                hots = [hot[blk, pl.ds((r * 5 + e) * BLK + at, 32), :] for r, e, _ in taps_here]
                for b in range(NBAS):
                    total = None
                    for h, (_, _, k) in zip(hots, taps_here, strict=True):
                        tap = splat[k * NBAS + b]
                        tap = jnp.concatenate([tap, tap], axis=0)
                        tap = jnp.concatenate([tap, tap], axis=1)
                        total = tap * h if total is None else total + tap * h
                    sel[blk // 2, pl.ds(b * BLK + at, 32), pl.ds(i * COLS, COLS)] = total
                return 0

            lax.fori_loop(0, BLK // 32, some, 0)

    def halo_matrix():
        spread = ones_where(iota((NBAS * 16, NBAS), 0) // 16 == iota((NBAS * 16, NBAS), 1))
        tall = lax.dot_general(spread, taps(), NT, preferred_element_type=F32).astype(BF16)
        tap, column = iota((50, 1024), 0), iota((50, 1024), 1)
        i_t, a, e = tap % 2, tap // 10 - 2, (tap // 2) % 5 - 2
        to, cell = column // 128, column % 128
        i_out, out_col = to // 4, jnp.where(to % 4 < 2, to % 4, to % 4 + COLS - 4)
        within = cell % 16
        cell_row = jnp.where(cell < 16, 0, jnp.where(cell < 32, -2, 2)) + (within % 4) // 2
        cell_col = jnp.where(within < 4, COLS, -2) + within % 2
        real = jnp.logical_and(cell < 48, within < 8)
        match = jnp.logical_and(i_t == i_out, cell_row - i_out == a)
        match = jnp.logical_and(match, cell_col - out_col == e)
        match = jnp.logical_and(jnp.logical_and(match, real), inside(cell_row))
        every = jnp.dot(tall, ones_where(match), preferred_element_type=F32)
        line = iota((NBAS * 16, 128), 0) % 16
        mine = jnp.zeros((NBAS * 16, 128), F32)
        for to in range(8):
            mine = jnp.where(line == to, every[:, to * 128 : (to + 1) * 128], mine)
        for b in range(NBAS):
            hsel[:, b * 128 : (b + 1) * 128] = mine[b * 16 : (b + 1) * 16].astype(BF16)

    def keys_values(first, count, start=0, height=BLK):
        part = pl.ds(start, height)
        x = jnp.concatenate([slots[first + n, part] for n in range(count)], axis=0)
        kv = jnp.dot(x, wqkv[:, D:], preferred_element_type=F32).astype(BF16)
        for n in range(count):
            kb[CODE[first + n], part] = kv[n * height : (n + 1) * height, :D]
            vb[CODE[first + n], part] = kv[n * height : (n + 1) * height, D:]

    loads[3].wait()
    loads[4].wait()
    loads[9].wait()
    one_hots(1)
    tap_matrices()
    halo_matrix()
    spread_taps()
    relay(0)

    loads[5].wait()
    scale = math.log2(math.e) / math.sqrt(D // HEADS)
    projected = jnp.dot(slots[OWN], wqkv[...], preferred_element_type=F32)
    qb[...] = (projected[:, :D] * scale).astype(BF16)
    kb[CODE[OWN]] = projected[:, D : 2 * D].astype(BF16)
    vb[CODE[OWN]] = projected[:, 2 * D :].astype(BF16)

    relay(1)
    pl.when(has_down)(lambda: wait_all([C_AUP]))
    pl.when(has_up)(lambda: wait_all([C_ADOWN]))
    one_hots(0)
    one_hots(2)
    relay(2)
    selections(0)
    relay(3)
    keys_values(LEFT, 2)
    pl.when(has_down)(lambda: wait_all([C_UP]))
    pl.when(has_up)(lambda: wait_all([C_DOWN]))
    keys_values(UP, 2)
    selections(2)

    head_lane = iota((BLK, 128), 1) // 32
    zero = jnp.zeros((BLK, 128), BF16)

    def attend(part, keys, vals):
        q = qb[:, part]
        wide = jnp.concatenate([jnp.where(head_lane == h, q, zero) for h in range(4)], axis=0)
        scores = lax.dot_general(wide, keys, NT, preferred_element_type=F32)
        top = jnp.max(scores, axis=-1, keepdims=True)
        weights = jnp.exp2(scores - top).astype(BF16)
        ones = jnp.ones(vals.shape, BF16)
        summed = jnp.dot(
            weights, jnp.concatenate([vals, ones], axis=1), preferred_element_type=F32
        )
        num, den = summed[:BLK, :128], summed[:BLK, 128:]
        most = jnp.broadcast_to(top[:BLK], (BLK, 128))
        for h in range(1, 4):
            mine, rows = head_lane == h, slice(h * BLK, (h + 1) * BLK)
            num = jnp.where(mine, summed[rows, :128], num)
            den = jnp.where(mine, summed[rows, 128:], den)
            most = jnp.where(mine, top[rows], most)
        return num, den, most

    for g in range(4):
        part = pl.ds(g * 128, 128)
        own_num[:, part], own_den[:, part], own_top[:, part] = attend(
            part, kb[CODE[OWN], :, part], vb[CODE[OWN], :, part]
        )

    loads[6].wait()
    for o in range(OUTP // 16):
        for b in range(NBAS):
            piece = wdec[b, o * 16 : min(o * 16 + 16, OUT)]
            if piece.shape[0] < 16:
                piece = jnp.concatenate([piece, jnp.zeros((16 - piece.shape[0], D), BF16)], axis=0)
            at = (o * NBAS + b) * 16
            wtp[at : at + 16] = piece

    own = asg[1] & (BLK - 1)
    lane1 = lax.broadcasted_iota(jnp.int32, (8, 128), 1)
    marks = jnp.full((8, 128), -1, jnp.int32)
    for r in range(2):
        for side in range(2):
            piece = jnp.broadcast_to(own[r : r + 1, side * 128 : side * 128 + 128], (8, 128))
            first, source = 4 * side + 2 * r, 126 * side
            moved = pltpu.roll(piece, (first - source) % 128, 1) if first != source else piece
            marks = jnp.where(jnp.logical_and(lane1 >= first, lane1 < first + 2), moved, marks)
    tall = jnp.concatenate([marks] * (BLK // 8), axis=0)
    hits = jnp.where(node[:, :128] == tall, 1.0, 0.0)
    onehot_e[...] = jnp.transpose(hits)[:16].astype(BF16)

    for half in range(2):
        chunks = range(half * CHUNKS // 2, (half + 1) * CHUNKS // 2)
        from_down, from_up = (
            [C_DIAG + 4 * c + 2 * side + v for c in chunks for side in (0, 1)] for v in (0, 1)
        )
        pl.when(has_down)(lambda keys=from_down: wait_all(keys))
        pl.when(has_up)(lambda keys=from_up: wait_all(keys))
        keys_values(UL, 4, half * (BLK // 2), BLK // 2)

    slot = []
    for n in range(1, 5):
        there = nbr[0, n]
        row_step = there // n_lon - reg
        col_step = lax.rem(there % n_lon - lon + 1 + n_lon, n_lon) - 1
        code = (row_step + 1) * 3 + col_step + 1
        slot.append(jnp.clip(code, 0, 8))
    for g in range(4):
        part = pl.ds(g * 128, 128)
        keys = jnp.concatenate([kb[s, :, part] for s in slot], axis=0)
        vals = jnp.concatenate([vb[s, :, part] for s in slot], axis=0)
        num, den, top = attend(part, keys, vals)
        first = own_top[:, part]
        both = jnp.maximum(first, top)
        old, new = jnp.exp2(first - both), jnp.exp2(top - both)
        num = num * new + own_num[:, part] * old
        den = den * new + own_den[:, part] * old
        att[:, part] = (num / den).astype(BF16)

    loads[7].wait()
    loads[8].wait()
    state = (
        xs[...].astype(F32) + jnp.dot(att[...], wout[...], preferred_element_type=F32)
    ).astype(BF16)
    state_o[...] = state
    v = jnp.dot(state, wlat[...], preferred_element_type=F32)
    lat[1] = (v / (1.0 + jnp.exp(-v))).astype(BF16)

    edge[...] = jnp.dot(onehot_e[...], lat[1], preferred_element_type=F32).astype(BF16)
    for n, (to, there) in enumerate(zip([left, right, *corners], (0, 1, 4, 5, 2, 3), strict=True)):
        copies[C_EDGE + n] = remote(C_EDGE + n, edge, edges_in.at[there], to)
    copies[C_LUP] = remote(C_LUP, lat.at[1], lat.at[2], up)
    copies[C_LDOWN] = remote(C_LDOWN, lat.at[1], lat.at[0], down)
    start_all([C_EDGE, C_EDGE + 1])
    pl.when(has_up)(lambda: start_all([C_EDGE + 2, C_EDGE + 3, C_LUP]))
    pl.when(has_down)(lambda: start_all([C_EDGE + 4, C_EDGE + 5, C_LDOWN]))
    upward.extend([C_EDGE + 2, C_EDGE + 3, C_LUP])
    downward.extend([C_EDGE + 4, C_EDGE + 5, C_LDOWN])

    def mixed(nodes_in):
        return lax.dot_general(wtp[...], nodes_in, NT, preferred_element_type=F32).astype(BF16)

    n_out = OUTP // 16
    high = NBAS * 16

    def decode_own():
        z = mixed(lat[1])
        z = jnp.concatenate([z[o * high : (o + 1) * high] for o in range(n_out)], axis=1)
        w = jnp.dot(kron[...], z, preferred_element_type=F32).astype(BF16)
        pieces = []
        for i in range(2):
            for o in range(n_out):
                line = [w[(i * 10 + k) * 16 : (i * 10 + k + 1) * 16, o * 128 : (o + 1) * 128] for k in range(10)]
                pieces.append(jnp.concatenate(line, axis=1))
        return jnp.dot(jnp.concatenate(pieces, axis=0), hot[1], preferred_element_type=F32)

    def by_output(z):
        lines = [
            jnp.concatenate([z[o * high + b * 16 : o * high + b * 16 + 16] for b in range(NBAS)], axis=1)
            for o in range(n_out)
        ]
        return jnp.concatenate(lines, axis=0)

    def decode_far(z, k):
        return jnp.dot(by_output(z), sel[k], preferred_element_type=F32)

    total = decode_own()

    even = lax.rem(reg, 2) == 0
    has_far = jnp.logical_or(jnp.logical_and(even, has_up), jnp.logical_and(reg % 2 == 1, has_down))
    near = jnp.where(even, 1, 0)
    other[...] = jnp.zeros((OUTP, 2 * COLS), F32)

    def add_block(n, _):
        k = jnp.where(n == 0, near, 1 - near)

        @pl.when(jnp.logical_or(n == 0, has_far))
        def _():
            remote(C_LUP + 1 - k, lat.at[1], lat.at[k * 2], up).wait_recv()

        other[...] += decode_far(mixed(lat[k * 2]), k)
        return 0

    lax.fori_loop(0, 2, add_block, 0)
    wait_all([C_EDGE, C_EDGE + 1])
    pl.when(has_down)(lambda: wait_all([C_EDGE + 2, C_EDGE + 3]))
    pl.when(has_up)(lambda: wait_all([C_EDGE + 4, C_EDGE + 5]))
    first4 = iota((16, D), 0) < 4
    cells = []
    for n in range(3):
        a, b = edges_in[2 * n], edges_in[2 * n + 1]
        cells.append(jnp.where(first4, a, b))
    z = by_output(mixed(jnp.concatenate(cells + [jnp.zeros((80, D), BF16)], axis=0)))
    sides = lax.dot_general(z, hsel[...], NT, preferred_element_type=F32)
    sides = jnp.concatenate([sides, jnp.zeros((OUTP, 112), F32)], axis=1)
    lane2 = iota((OUTP, 128), 1)
    for i in range(2):
        at_left = pltpu.roll(sides, (-4 * i) % 128, 1) if i else sides
        at_left = jnp.where(lane2 < 2, at_left, 0.0)
        at_right = jnp.where(lane2 >= 126, pltpu.roll(sides, 124 - 4 * i, 1), 0.0)
        whole = total[i * OUTP : (i + 1) * OUTP] + other[:, i * COLS : (i + 1) * COLS]
        whole += jnp.concatenate([at_left, at_right], axis=1)
        fields_o[:, i, :] = whole[:OUT].astype(BF16)

    def sent(keys):
        for k in keys:
            copies[k].wait_send()

    sent([k for k in copies if k not in upward and k not in downward])
    pl.when(has_up)(lambda: sent(upward))
    pl.when(has_down)(lambda: sent(downward))


def store(state, fields, state_o, fields_o, sem):
    copies = [
        pltpu.make_async_copy(state, state_o, sem.at[0]),
        pltpu.make_async_copy(fields, fields_o, sem.at[1]),
    ]
    for copy in copies:
        copy.start()
    for copy in copies:
        copy.wait()


def shards(sizes, nodes, norm_gain, w_qkv, w_out, w_latent, neighbours, assignment, psi, w_dec):
    anywhere = pl.BlockSpec(memory_space=pl.ANY)
    vmem = pl.BlockSpec(memory_space=pltpu.VMEM)
    state, fields = pl.pallas_call(
        functools.partial(kernel, *sizes),
        out_shape=(
            pltpu.VMEM((BLK, D), BF16),
            pltpu.VMEM((OUT, 2, COLS), BF16),
        ),
        in_specs=[anywhere] * 9,
        out_specs=(vmem, vmem),
        scratch_shapes=[
            pltpu.VMEM((BLK, D), BF16),
            pltpu.VMEM((1, D), F32),
            pltpu.VMEM((D, 3 * D), BF16),
            pltpu.VMEM((D, D), BF16),
            pltpu.VMEM((D, D), BF16),
            pltpu.SMEM((1, 5), jnp.int32),
            pltpu.VMEM((3, 2, COLS), jnp.int32),
            pltpu.VMEM((5, 5, 2, NBAS), F32),
            pltpu.SMEM((5, 5, 2, NBAS), F32),
            pltpu.VMEM((NBAS, OUT, D), BF16),
            pltpu.VMEM((NBAS * OUTP, D), BF16),
            pltpu.VMEM((9, BLK, D), BF16),
            pltpu.VMEM((BLK, D), BF16),
            pltpu.VMEM((9, BLK, D), BF16),
            pltpu.VMEM((9, BLK, D), BF16),
            pltpu.VMEM((BLK, D), F32),
            pltpu.VMEM((BLK, D), F32),
            pltpu.VMEM((BLK, D), F32),
            pltpu.VMEM((BLK, D), BF16),
            pltpu.VMEM((3, BLK, D), BF16),
            pltpu.VMEM((16, D), BF16),
            pltpu.VMEM((6, 16, D), BF16),
            pltpu.VMEM((16, 128), BF16),
            pltpu.VMEM((3, 10 * BLK, COLS), BF16),
            pltpu.VMEM((320, NBAS * 16), BF16),
            pltpu.VMEM((16, NBAS * 128), BF16),
            pltpu.VMEM((30 * NBAS, 16, 128), BF16),
            pltpu.VMEM((2, NBAS * BLK, 2 * COLS), BF16),
            pltpu.VMEM((OUTP, 2 * COLS), F32),
            pltpu.SemaphoreType.DMA((10,)),
            pltpu.SemaphoreType.DMA((N_COPIES,)),
            pltpu.SemaphoreType.DMA((N_COPIES,)),
        ],
        compiler_params=pltpu.CompilerParams(
            collective_id=0, has_side_effects=True, vmem_limit_bytes=56 * 2**20
        ),
    )(
        nodes[0], norm_gain[None], w_qkv, w_out, w_latent, neighbours, assignment,
        psi.transpose(2, 3, 1, 0), w_dec.transpose(0, 2, 1),
    )
    state, fields = pl.pallas_call(
        store,
        out_shape=(
            jax.ShapeDtypeStruct((BLK, D), BF16),
            jax.ShapeDtypeStruct((OUT, 2, COLS), BF16),
        ),
        in_specs=[vmem] * 2,
        out_specs=(anywhere, anywhere),
        scratch_shapes=[pltpu.SemaphoreType.DMA((2,))],
    )(
        pltpu.with_memory_space_constraint(state, pltpu.VMEM),
        pltpu.with_memory_space_constraint(fields, pltpu.VMEM),
    )
    return state[None], fields[None]


def solution(mesh):
    sizes = (mesh.shape["reg"], mesh.shape["lon"])
    in_specs = (
        P(None, ("reg", "lon"), None),
        P(),
        P(),
        P(),
        P(),
        P(("reg", "lon"), None),
        P("reg", "lon"),
        P(None, "reg", None, None),
        P(),
    )
    out_specs = (P(None, ("reg", "lon"), None), P(None, None, "reg", "lon"))
    return jax.shard_map(
        functools.partial(shards, sizes),
        mesh=mesh,
        in_specs=in_specs,
        out_specs=out_specs,
        check_vma=False,
    )
```

```python
import functools
import math

import jax
import jax.numpy as jnp
from jax import lax
from jax.experimental import pallas as pl
from jax.experimental.pallas import tpu as pltpu
from jax.sharding import PartitionSpec as P

MESH = pl.DeviceIdType.MESH
F32, BF16 = jnp.float32, jnp.bfloat16
HEADS = 16
CHUNKS = 4
BLK, D = 128, 512
COLS = 256
NBAS, OUT, OUTP = 9, 84, 96
NT = (((1,), (1,)), ((), ()))
FAR = [(0, -2), (0, -1), (1, -2), (0, 2), (1, 1), (1, 2)]

OWN, LEFT, RIGHT, UP, DOWN, UL, UR, DL, DR = range(9)
STEPS = [(0, 0), (0, -1), (0, 1), (-1, 0), (1, 0), (-1, -1), (-1, 1), (1, -1), (1, 1)]
CODE = [(r + 1) * 3 + c + 1 for r, c in STEPS]

C_UP, C_DOWN, C_AUP, C_ADOWN, C_LUP, C_LDOWN = range(6)
C_EDGE = 6
C_LON = 12
C_DIAG = C_LON + 2 * CHUNKS
N_COPIES = C_DIAG + 4 * CHUNKS


def kernel(
    n_reg, n_lon,
    nodes_h, gain_h, wqkv_h, wout_h, wlat_h, nbr_h, asg_h, psi_h, wdec_h,
    state_o, fields_o,
    xs, gain, wqkv, wout, wlat, nbr, asg, psi, psi_s, wdec, wtp,
    slots, qb, kb, vb, own_num, own_den, own_top, att, lat, edge, edges_in, onehot_e,
    hot, kron, hsel, splat, sel, other,
    load_sem, send_sem, recv_sem,
):
    reg, lon = lax.axis_index("reg"), lax.axis_index("lon")
    up = (lax.rem(reg + n_reg - 1, n_reg), lon)
    down = (lax.rem(reg + 1, n_reg), lon)
    left = (reg, lax.rem(lon + n_lon - 1, n_lon))
    right = (reg, lax.rem(lon + 1, n_lon))
    corners = [(v[0], h[1]) for v in (up, down) for h in (left, right)]

    has_up, has_down = reg > 0, reg < n_reg - 1

    barrier = pltpu.get_barrier_semaphore()

    def greet(where):
        pl.semaphore_signal(barrier, inc=1, device_id=where, device_id_type=MESH)

    greet(left)
    greet(right)
    pl.when(has_up)(lambda: greet(up))
    pl.when(has_down)(lambda: greet(down))

    loads = [
        pltpu.make_async_copy(src, dst, load_sem.at[k])
        for k, (src, dst) in enumerate(
            [(nodes_h, xs), (gain_h, gain), (asg_h, asg.at[1]), (psi_h, psi), (nbr_h, nbr),
             (wqkv_h, wqkv), (wdec_h, wdec), (wout_h, wout), (wlat_h, wlat), (psi_h, psi_s)]
        )
    ]
    for load in loads:
        load.start()

    def remote(k, src, dst, to):
        return pltpu.make_async_remote_copy(
            src_ref=src, dst_ref=dst, send_sem=send_sem.at[k], recv_sem=recv_sem.at[k],
            device_id=to, device_id_type=MESH,
        )

    loads[0].wait()
    loads[1].wait()
    values = xs[...].astype(F32)
    center = values - jnp.mean(values, axis=-1, keepdims=True)
    spread = jnp.mean(center * center, axis=-1, keepdims=True)
    slots[OWN] = (center * lax.rsqrt(spread + 1e-05) * gain[...]).astype(BF16)
    loads[2].wait()

    pl.semaphore_wait(barrier, 2 + has_up.astype(jnp.int32) + has_down.astype(jnp.int32))

    rows = BLK // CHUNKS
    copies = {}
    for c in range(CHUNKS):
        part = pl.ds(c * rows, rows)
        for side, (to, slot) in enumerate(((left, RIGHT), (right, LEFT))):
            k = C_LON + 2 * c + side
            copies[k] = remote(k, slots.at[OWN, part], slots.at[slot, part], to)
            copies[k].start()
    copies[C_UP] = remote(C_UP, slots.at[OWN], slots.at[DOWN], up)
    copies[C_DOWN] = remote(C_DOWN, slots.at[OWN], slots.at[UP], down)
    copies[C_AUP] = remote(C_AUP, asg.at[1], asg.at[2], up)
    copies[C_ADOWN] = remote(C_ADOWN, asg.at[1], asg.at[0], down)

    upward, downward = [C_UP, C_AUP], [C_DOWN, C_ADOWN]

    def start_all(keys):
        for k in keys:
            copies[k].start()

    def wait_all(keys):
        for k in keys:
            copies[k].wait_recv()

    pl.when(has_up)(lambda: start_all([C_UP, C_AUP]))
    pl.when(has_down)(lambda: start_all([C_DOWN, C_ADOWN]))

    def clear(blk):
        lat[blk] = jnp.zeros((BLK, D), BF16)
        asg[blk] = jnp.zeros((2, COLS), jnp.int32)
        for n in (0, 1):
            edges_in[blk + 2 + n] = jnp.zeros((16, D), BF16)
        for slot in (UP, UL, UR) if blk == 0 else (DOWN, DL, DR):
            slots[slot] = jnp.zeros((BLK, D), BF16)

    pl.when(jnp.logical_not(has_up))(lambda: clear(0))
    pl.when(jnp.logical_not(has_down))(lambda: clear(2))

    def relay(c):
        part = pl.ds(c * rows, rows)
        for side, (slot, to_up, to_down) in enumerate(((RIGHT, DR, UR), (LEFT, DL, UL))):
            copies[C_LON + 2 * c + side].wait_recv()
            for v, (to, there) in enumerate(((up, to_up), (down, to_down))):
                k = C_DIAG + 4 * c + 2 * side + v
                copies[k] = remote(k, slots.at[slot, part], slots.at[there, part], to)
        ups, downs = ([C_DIAG + 4 * c + 2 * side + v for side in (0, 1)] for v in (0, 1))
        upward.extend(ups)
        downward.extend(downs)
        pl.when(has_up)(lambda: start_all(ups))
        pl.when(has_down)(lambda: start_all(downs))

    lane = lax.broadcasted_iota(jnp.int32, (8, COLS), 1)
    node = lax.broadcasted_iota(jnp.int32, (BLK, COLS), 0)

    def one_hots(blk):
        for r in range(2):
            local = jnp.broadcast_to(asg[blk, r : r + 1, :] & (BLK - 1), (8, COLS))
            for e in range(5):
                s = e - 2
                moved = pltpu.roll(local, (-s) % COLS, 1) if s else local
                if s < 0:
                    moved = jnp.where(lane < -s, -1, moved)
                if s > 0:
                    moved = jnp.where(lane >= COLS - s, -1, moved)
                tall = jnp.concatenate([moved] * (BLK // 8), axis=0)
                at = (r * 5 + e) * BLK
                hot[blk, at : at + BLK] = jnp.where(node == tall, 1.0, 0.0).astype(BF16)

    def iota(shape, dim):
        return lax.broadcasted_iota(jnp.int32, shape, dim)

    def ones_where(condition):
        return jnp.where(condition, 1.0, 0.0).astype(BF16)

    def inside(row):
        row = row + 2 * reg
        return jnp.logical_and(row >= 0, row < 2 * n_reg)

    def taps():
        return psi[...].reshape(50, NBAS).astype(BF16)

    def tap_matrices():
        spread = ones_where(iota((NBAS, NBAS * 16), 0) == iota((NBAS, NBAS * 16), 1) // 16)
        wide = jnp.dot(taps(), spread, preferred_element_type=F32).astype(BF16)
        line, tap = iota((320, 50), 0) // 16, iota((320, 50), 1)
        i, r, e = line // 10, (line // 5) % 2, line % 5
        diagonal = iota((320, NBAS * 16), 0) % 16 == iota((320, NBAS * 16), 1) % 16
        pick = ones_where(tap == ((r - i + 2) * 5 + e) * 2 + i)
        full = jnp.dot(pick, wide, preferred_element_type=F32)
        kron[...] = jnp.where(diagonal, full, 0.0).astype(BF16)

    def spread_taps():
        for n, (i, a) in enumerate(FAR):

            def at_step(e, _, n=n, i=i, a=a):
                for b in range(NBAS):
                    tap = jnp.where(inside(i + a), psi_s[a + 2, e, i, b], 0.0)
                    splat[(n * 5 + e) * NBAS + b] = jnp.full((16, 128), tap, F32).astype(BF16)
                return 0

            lax.fori_loop(0, 5, at_step, 0)

    def selections(blk):
        for i in range(2):
            taps_here = [
                (r, e, FAR.index((i, a)) * 5 + e)
                for r, a in ((r, 2 * (blk - 1) + r - i) for r in range(2))
                if (i, a) in FAR
                for e in range(5)
            ]

            def some(n, _, i=i, taps_here=taps_here):
                at = pl.multiple_of(n * 32, 32)
                hots = [hot[blk, pl.ds((r * 5 + e) * BLK + at, 32), :] for r, e, _ in taps_here]
                for b in range(NBAS):
                    total = None
                    for h, (_, _, k) in zip(hots, taps_here, strict=True):
                        tap = splat[k * NBAS + b]
                        tap = jnp.concatenate([tap, tap], axis=0)
                        tap = jnp.concatenate([tap, tap], axis=1)
                        total = tap * h if total is None else total + tap * h
                    sel[blk // 2, pl.ds(b * BLK + at, 32), pl.ds(i * COLS, COLS)] = total
                return 0

            lax.fori_loop(0, BLK // 32, some, 0)

    def halo_matrix():
        spread = ones_where(iota((NBAS * 16, NBAS), 0) // 16 == iota((NBAS * 16, NBAS), 1))
        tall = lax.dot_general(spread, taps(), NT, preferred_element_type=F32).astype(BF16)
        tap, column = iota((50, 1024), 0), iota((50, 1024), 1)
        i_t, a, e = tap % 2, tap // 10 - 2, (tap // 2) % 5 - 2
        to, cell = column // 128, column % 128
        i_out, out_col = to // 4, jnp.where(to % 4 < 2, to % 4, to % 4 + COLS - 4)
        within = cell % 16
        cell_row = jnp.where(cell < 16, 0, jnp.where(cell < 32, -2, 2)) + (within % 4) // 2
        cell_col = jnp.where(within < 4, COLS, -2) + within % 2
        real = jnp.logical_and(cell < 48, within < 8)
        match = jnp.logical_and(i_t == i_out, cell_row - i_out == a)
        match = jnp.logical_and(match, cell_col - out_col == e)
        match = jnp.logical_and(jnp.logical_and(match, real), inside(cell_row))
        every = jnp.dot(tall, ones_where(match), preferred_element_type=F32)
        line = iota((NBAS * 16, 128), 0) % 16
        mine = jnp.zeros((NBAS * 16, 128), F32)
        for to in range(8):
            mine = jnp.where(line == to, every[:, to * 128 : (to + 1) * 128], mine)
        for b in range(NBAS):
            hsel[:, b * 128 : (b + 1) * 128] = mine[b * 16 : (b + 1) * 16].astype(BF16)

    def keys_values(first, count, start=0, height=BLK):
        part = pl.ds(start, height)
        x = jnp.concatenate([slots[first + n, part] for n in range(count)], axis=0)
        kv = jnp.dot(x, wqkv[:, D:], preferred_element_type=F32).astype(BF16)
        for n in range(count):
            kb[CODE[first + n], part] = kv[n * height : (n + 1) * height, :D]
            vb[CODE[first + n], part] = kv[n * height : (n + 1) * height, D:]

    loads[3].wait()
    loads[4].wait()
    loads[9].wait()
    one_hots(1)
    tap_matrices()
    halo_matrix()
    spread_taps()
    relay(0)

    loads[5].wait()
    scale = math.log2(math.e) / math.sqrt(D // HEADS)
    projected = jnp.dot(slots[OWN], wqkv[...], preferred_element_type=F32)
    qb[...] = (projected[:, :D] * scale).astype(BF16)
    kb[CODE[OWN]] = projected[:, D : 2 * D].astype(BF16)
    vb[CODE[OWN]] = projected[:, 2 * D :].astype(BF16)

    relay(1)
    pl.when(has_down)(lambda: wait_all([C_AUP]))
    pl.when(has_up)(lambda: wait_all([C_ADOWN]))
    one_hots(0)
    one_hots(2)
    relay(2)
    selections(0)
    relay(3)
    keys_values(LEFT, 2)
    pl.when(has_down)(lambda: wait_all([C_UP]))
    pl.when(has_up)(lambda: wait_all([C_DOWN]))
    keys_values(UP, 2)
    selections(2)

    head_lane = iota((BLK, 128), 1) // 32
    zero = jnp.zeros((BLK, 128), BF16)

    def attend(part, keys, vals):
        q = qb[:, part]
        wide = jnp.concatenate([jnp.where(head_lane == h, q, zero) for h in range(4)], axis=0)
        scores = lax.dot_general(wide, keys, NT, preferred_element_type=F32)
        top = jnp.max(scores, axis=-1, keepdims=True)
        weights = jnp.exp2(scores - top).astype(BF16)
        ones = jnp.ones(vals.shape, BF16)
        summed = jnp.dot(
            weights, jnp.concatenate([vals, ones], axis=1), preferred_element_type=F32
        )
        num, den = summed[:BLK, :128], summed[:BLK, 128:]
        most = jnp.broadcast_to(top[:BLK], (BLK, 128))
        for h in range(1, 4):
            mine, rows = head_lane == h, slice(h * BLK, (h + 1) * BLK)
            num = jnp.where(mine, summed[rows, :128], num)
            den = jnp.where(mine, summed[rows, 128:], den)
            most = jnp.where(mine, top[rows], most)
        return num, den, most

    for g in range(4):
        part = pl.ds(g * 128, 128)
        own_num[:, part], own_den[:, part], own_top[:, part] = attend(
            part, kb[CODE[OWN], :, part], vb[CODE[OWN], :, part]
        )

    loads[6].wait()
    for o in range(OUTP // 16):
        for b in range(NBAS):
            piece = wdec[b, o * 16 : min(o * 16 + 16, OUT)]
            if piece.shape[0] < 16:
                piece = jnp.concatenate([piece, jnp.zeros((16 - piece.shape[0], D), BF16)], axis=0)
            at = (o * NBAS + b) * 16
            wtp[at : at + 16] = piece

    own = asg[1] & (BLK - 1)
    lane1 = lax.broadcasted_iota(jnp.int32, (8, 128), 1)
    marks = jnp.full((8, 128), -1, jnp.int32)
    for r in range(2):
        for side in range(2):
            piece = jnp.broadcast_to(own[r : r + 1, side * 128 : side * 128 + 128], (8, 128))
            first, source = 4 * side + 2 * r, 126 * side
            moved = pltpu.roll(piece, (first - source) % 128, 1) if first != source else piece
            marks = jnp.where(jnp.logical_and(lane1 >= first, lane1 < first + 2), moved, marks)
    tall = jnp.concatenate([marks] * (BLK // 8), axis=0)
    hits = jnp.where(node[:, :128] == tall, 1.0, 0.0)
    onehot_e[...] = jnp.transpose(hits)[:16].astype(BF16)

    for chunks in (range(CHUNKS - 1), range(CHUNKS - 1, CHUNKS)):
        from_down, from_up = (
            [C_DIAG + 4 * c + 2 * side + v for c in chunks for side in (0, 1)] for v in (0, 1)
        )
        pl.when(has_down)(lambda keys=from_down: wait_all(keys))
        pl.when(has_up)(lambda keys=from_up: wait_all(keys))
        keys_values(UL, 4, chunks[0] * rows, len(chunks) * rows)

    slot = []
    for n in range(1, 5):
        there = nbr[0, n]
        row_step = there // n_lon - reg
        col_step = lax.rem(there % n_lon - lon + 1 + n_lon, n_lon) - 1
        code = (row_step + 1) * 3 + col_step + 1
        slot.append(jnp.clip(code, 0, 8))
    for g in range(4):
        part = pl.ds(g * 128, 128)
        keys = jnp.concatenate([kb[s, :, part] for s in slot], axis=0)
        vals = jnp.concatenate([vb[s, :, part] for s in slot], axis=0)
        num, den, top = attend(part, keys, vals)
        first = own_top[:, part]
        both = jnp.maximum(first, top)
        old, new = jnp.exp2(first - both), jnp.exp2(top - both)
        num = num * new + own_num[:, part] * old
        den = den * new + own_den[:, part] * old
        att[:, part] = (num / den).astype(BF16)

    loads[7].wait()
    loads[8].wait()
    state = (
        xs[...].astype(F32) + jnp.dot(att[...], wout[...], preferred_element_type=F32)
    ).astype(BF16)
    state_o[...] = state
    v = jnp.dot(state, wlat[...], preferred_element_type=F32)
    lat[1] = (v / (1.0 + jnp.exp(-v))).astype(BF16)

    edge[...] = jnp.dot(onehot_e[...], lat[1], preferred_element_type=F32).astype(BF16)
    for n, (to, there) in enumerate(zip([left, right, *corners], (0, 1, 4, 5, 2, 3), strict=True)):
        copies[C_EDGE + n] = remote(C_EDGE + n, edge, edges_in.at[there], to)
    copies[C_LUP] = remote(C_LUP, lat.at[1], lat.at[2], up)
    copies[C_LDOWN] = remote(C_LDOWN, lat.at[1], lat.at[0], down)
    pl.when(has_up)(lambda: start_all([C_EDGE + 2, C_EDGE + 3]))
    pl.when(has_down)(lambda: start_all([C_EDGE + 4, C_EDGE + 5]))
    start_all([C_EDGE, C_EDGE + 1])
    pl.when(has_up)(lambda: start_all([C_LUP]))
    pl.when(has_down)(lambda: start_all([C_LDOWN]))
    upward.extend([C_EDGE + 2, C_EDGE + 3, C_LUP])
    downward.extend([C_EDGE + 4, C_EDGE + 5, C_LDOWN])

    def mixed(nodes_in):
        return lax.dot_general(wtp[...], nodes_in, NT, preferred_element_type=F32).astype(BF16)

    n_out = OUTP // 16
    high = NBAS * 16

    def decode_own():
        z = mixed(lat[1])
        z = jnp.concatenate([z[o * high : (o + 1) * high] for o in range(n_out)], axis=1)
        w = jnp.dot(kron[...], z, preferred_element_type=F32).astype(BF16)
        pieces = []
        for i in range(2):
            for o in range(n_out):
                line = [w[(i * 10 + k) * 16 : (i * 10 + k + 1) * 16, o * 128 : (o + 1) * 128] for k in range(10)]
                pieces.append(jnp.concatenate(line, axis=1))
        return jnp.dot(jnp.concatenate(pieces, axis=0), hot[1], preferred_element_type=F32)

    def by_output(z):
        lines = [
            jnp.concatenate([z[o * high + b * 16 : o * high + b * 16 + 16] for b in range(NBAS)], axis=1)
            for o in range(n_out)
        ]
        return jnp.concatenate(lines, axis=0)

    def decode_far(z, k):
        return jnp.dot(by_output(z), sel[k], preferred_element_type=F32)

    total = decode_own()

    even = lax.rem(reg, 2) == 0
    has_far = jnp.logical_or(jnp.logical_and(even, has_up), jnp.logical_and(reg % 2 == 1, has_down))
    near = jnp.where(even, 1, 0)
    other[...] = jnp.zeros((OUTP, 2 * COLS), F32)

    def add_block(n, _):
        k = jnp.where(n == 0, near, 1 - near)

        @pl.when(jnp.logical_or(n == 0, has_far))
        def _():
            remote(C_LUP + 1 - k, lat.at[1], lat.at[k * 2], up).wait_recv()

        other[...] += decode_far(mixed(lat[k * 2]), k)
        return 0

    lax.fori_loop(0, 2, add_block, 0)
    wait_all([C_EDGE, C_EDGE + 1])
    pl.when(has_down)(lambda: wait_all([C_EDGE + 2, C_EDGE + 3]))
    pl.when(has_up)(lambda: wait_all([C_EDGE + 4, C_EDGE + 5]))
    first4 = iota((16, D), 0) < 4
    cells = []
    for n in range(3):
        a, b = edges_in[2 * n], edges_in[2 * n + 1]
        cells.append(jnp.where(first4, a, b))
    z = by_output(mixed(jnp.concatenate(cells + [jnp.zeros((80, D), BF16)], axis=0)))
    sides = lax.dot_general(z, hsel[...], NT, preferred_element_type=F32)
    sides = jnp.concatenate([sides, jnp.zeros((OUTP, 112), F32)], axis=1)
    lane2 = iota((OUTP, 128), 1)
    for i in range(2):
        at_left = pltpu.roll(sides, (-4 * i) % 128, 1) if i else sides
        at_left = jnp.where(lane2 < 2, at_left, 0.0)
        at_right = jnp.where(lane2 >= 126, pltpu.roll(sides, 124 - 4 * i, 1), 0.0)
        whole = total[i * OUTP : (i + 1) * OUTP] + other[:, i * COLS : (i + 1) * COLS]
        whole += jnp.concatenate([at_left, at_right], axis=1)
        fields_o[:, i, :] = whole[:OUT].astype(BF16)

    def sent(keys):
        for k in keys:
            copies[k].wait_send()

    sent([k for k in copies if k not in upward and k not in downward])
    pl.when(has_up)(lambda: sent(upward))
    pl.when(has_down)(lambda: sent(downward))


def store(state, fields, state_o, fields_o, sem):
    copies = [
        pltpu.make_async_copy(state, state_o, sem.at[0]),
        pltpu.make_async_copy(fields, fields_o, sem.at[1]),
    ]
    for copy in copies:
        copy.start()
    for copy in copies:
        copy.wait()


def shards(sizes, nodes, norm_gain, w_qkv, w_out, w_latent, neighbours, assignment, psi, w_dec):
    anywhere = pl.BlockSpec(memory_space=pl.ANY)
    vmem = pl.BlockSpec(memory_space=pltpu.VMEM)
    state, fields = pl.pallas_call(
        functools.partial(kernel, *sizes),
        out_shape=(
            pltpu.VMEM((BLK, D), BF16),
            pltpu.VMEM((OUT, 2, COLS), BF16),
        ),
        in_specs=[anywhere] * 9,
        out_specs=(vmem, vmem),
        scratch_shapes=[
            pltpu.VMEM((BLK, D), BF16),
            pltpu.VMEM((1, D), F32),
            pltpu.VMEM((D, 3 * D), BF16),
            pltpu.VMEM((D, D), BF16),
            pltpu.VMEM((D, D), BF16),
            pltpu.SMEM((1, 5), jnp.int32),
            pltpu.VMEM((3, 2, COLS), jnp.int32),
            pltpu.VMEM((5, 5, 2, NBAS), F32),
            pltpu.SMEM((5, 5, 2, NBAS), F32),
            pltpu.VMEM((NBAS, OUT, D), BF16),
            pltpu.VMEM((NBAS * OUTP, D), BF16),
            pltpu.VMEM((9, BLK, D), BF16),
            pltpu.VMEM((BLK, D), BF16),
            pltpu.VMEM((9, BLK, D), BF16),
            pltpu.VMEM((9, BLK, D), BF16),
            pltpu.VMEM((BLK, D), F32),
            pltpu.VMEM((BLK, D), F32),
            pltpu.VMEM((BLK, D), F32),
            pltpu.VMEM((BLK, D), BF16),
            pltpu.VMEM((3, BLK, D), BF16),
            pltpu.VMEM((16, D), BF16),
            pltpu.VMEM((6, 16, D), BF16),
            pltpu.VMEM((16, 128), BF16),
            pltpu.VMEM((3, 10 * BLK, COLS), BF16),
            pltpu.VMEM((320, NBAS * 16), BF16),
            pltpu.VMEM((16, NBAS * 128), BF16),
            pltpu.VMEM((30 * NBAS, 16, 128), BF16),
            pltpu.VMEM((2, NBAS * BLK, 2 * COLS), BF16),
            pltpu.VMEM((OUTP, 2 * COLS), F32),
            pltpu.SemaphoreType.DMA((10,)),
            pltpu.SemaphoreType.DMA((N_COPIES,)),
            pltpu.SemaphoreType.DMA((N_COPIES,)),
        ],
        compiler_params=pltpu.CompilerParams(
            collective_id=0, has_side_effects=True, vmem_limit_bytes=56 * 2**20
        ),
    )(
        nodes[0], norm_gain[None], w_qkv, w_out, w_latent, neighbours, assignment,
        psi.transpose(2, 3, 1, 0), w_dec.transpose(0, 2, 1),
    )
    state, fields = pl.pallas_call(
        store,
        out_shape=(
            jax.ShapeDtypeStruct((BLK, D), BF16),
            jax.ShapeDtypeStruct((OUT, 2, COLS), BF16),
        ),
        in_specs=[vmem] * 2,
        out_specs=(anywhere, anywhere),
        scratch_shapes=[pltpu.SemaphoreType.DMA((2,))],
    )(
        pltpu.with_memory_space_constraint(state, pltpu.VMEM),
        pltpu.with_memory_space_constraint(fields, pltpu.VMEM),
    )
    return state[None], fields[None]


def solution(mesh):
    sizes = (mesh.shape["reg"], mesh.shape["lon"])
    in_specs = (
        P(None, ("reg", "lon"), None),
        P(),
        P(),
        P(),
        P(),
        P(("reg", "lon"), None),
        P("reg", "lon"),
        P(None, "reg", None, None),
        P(),
    )
    out_specs = (P(None, ("reg", "lon"), None), P(None, None, "reg", "lon"))
    return jax.shard_map(
        functools.partial(shards, sizes),
        mesh=mesh,
        in_specs=in_specs,
        out_specs=out_specs,
        check_vma=False,
    )
```

```python
import functools
import math

import jax
import jax.numpy as jnp
from jax import lax
from jax.experimental import pallas as pl
from jax.experimental.pallas import tpu as pltpu
from jax.sharding import PartitionSpec as P

MESH = pl.DeviceIdType.MESH
F32, BF16 = jnp.float32, jnp.bfloat16
HEADS = 16
CHUNKS = 2
BLK, D = 128, 512
COLS = 256
NBAS, OUT, OUTP = 9, 84, 96
NT = (((1,), (1,)), ((), ()))
FAR = [(0, -2), (0, -1), (1, -2), (0, 2), (1, 1), (1, 2)]

OWN, LEFT, RIGHT, UP, DOWN, UL, UR, DL, DR = range(9)
STEPS = [(0, 0), (0, -1), (0, 1), (-1, 0), (1, 0), (-1, -1), (-1, 1), (1, -1), (1, 1)]
CODE = [(r + 1) * 3 + c + 1 for r, c in STEPS]

C_UP, C_DOWN, C_AUP, C_ADOWN, C_LUP, C_LDOWN = range(6)
C_EDGE = 6
C_LON = 12
C_DIAG = C_LON + 2 * CHUNKS
N_COPIES = C_DIAG + 4 * CHUNKS


def kernel(
    n_reg, n_lon,
    nodes_h, gain_h, wqkv_h, wout_h, wlat_h, nbr_h, asg_h, psi_h, wdec_h,
    state_o, fields_o,
    xs, gain, wqkv, wout, wlat, nbr, asg, psi, psi_s, wdec, wtp,
    slots, qb, kb, vb, own_num, own_den, own_top, att, lat, edge, edges_in, onehot_e,
    hot, kron, hsel, splat, sel, other,
    load_sem, send_sem, recv_sem,
):
    reg, lon = lax.axis_index("reg"), lax.axis_index("lon")
    up = (lax.rem(reg + n_reg - 1, n_reg), lon)
    down = (lax.rem(reg + 1, n_reg), lon)
    left = (reg, lax.rem(lon + n_lon - 1, n_lon))
    right = (reg, lax.rem(lon + 1, n_lon))
    corners = [(v[0], h[1]) for v in (up, down) for h in (left, right)]

    has_up, has_down = reg > 0, reg < n_reg - 1

    barrier = pltpu.get_barrier_semaphore()

    def greet(where):
        pl.semaphore_signal(barrier, inc=1, device_id=where, device_id_type=MESH)

    greet(left)
    greet(right)
    pl.when(has_up)(lambda: greet(up))
    pl.when(has_down)(lambda: greet(down))

    loads = [
        pltpu.make_async_copy(src, dst, load_sem.at[k])
        for k, (src, dst) in enumerate(
            [(nodes_h, xs), (gain_h, gain), (asg_h, asg.at[1]), (psi_h, psi), (nbr_h, nbr),
             (wqkv_h, wqkv), (wdec_h, wdec), (wout_h, wout), (wlat_h, wlat), (psi_h, psi_s)]
        )
    ]
    for load in loads:
        load.start()

    def remote(k, src, dst, to):
        return pltpu.make_async_remote_copy(
            src_ref=src, dst_ref=dst, send_sem=send_sem.at[k], recv_sem=recv_sem.at[k],
            device_id=to, device_id_type=MESH,
        )

    loads[0].wait()
    loads[1].wait()
    values = xs[...].astype(F32)
    center = values - jnp.mean(values, axis=-1, keepdims=True)
    spread = jnp.mean(center * center, axis=-1, keepdims=True)
    slots[OWN] = (center * lax.rsqrt(spread + 1e-05) * gain[...]).astype(BF16)
    loads[2].wait()

    pl.semaphore_wait(barrier, 2 + has_up.astype(jnp.int32) + has_down.astype(jnp.int32))

    rows = BLK // CHUNKS
    copies = {}
    for c in range(CHUNKS):
        part = pl.ds(c * rows, rows)
        for side, (to, slot) in enumerate(((left, RIGHT), (right, LEFT))):
            k = C_LON + 2 * c + side
            copies[k] = remote(k, slots.at[OWN, part], slots.at[slot, part], to)
            copies[k].start()
    copies[C_UP] = remote(C_UP, slots.at[OWN], slots.at[DOWN], up)
    copies[C_DOWN] = remote(C_DOWN, slots.at[OWN], slots.at[UP], down)
    copies[C_AUP] = remote(C_AUP, asg.at[1], asg.at[2], up)
    copies[C_ADOWN] = remote(C_ADOWN, asg.at[1], asg.at[0], down)

    upward, downward = [C_UP, C_AUP], [C_DOWN, C_ADOWN]

    def start_all(keys):
        for k in keys:
            copies[k].start()

    def wait_all(keys):
        for k in keys:
            copies[k].wait_recv()

    pl.when(has_up)(lambda: start_all([C_UP, C_AUP]))
    pl.when(has_down)(lambda: start_all([C_DOWN, C_ADOWN]))

    def clear(blk):
        lat[blk] = jnp.zeros((BLK, D), BF16)
        asg[blk] = jnp.zeros((2, COLS), jnp.int32)
        for n in (0, 1):
            edges_in[blk + 2 + n] = jnp.zeros((16, D), BF16)
        for slot in (UP, UL, UR) if blk == 0 else (DOWN, DL, DR):
            slots[slot] = jnp.zeros((BLK, D), BF16)

    pl.when(jnp.logical_not(has_up))(lambda: clear(0))
    pl.when(jnp.logical_not(has_down))(lambda: clear(2))

    def relay(c):
        part = pl.ds(c * rows, rows)
        for side, (slot, to_up, to_down) in enumerate(((RIGHT, DR, UR), (LEFT, DL, UL))):
            copies[C_LON + 2 * c + side].wait_recv()
            for v, (to, there) in enumerate(((up, to_up), (down, to_down))):
                k = C_DIAG + 4 * c + 2 * side + v
                copies[k] = remote(k, slots.at[slot, part], slots.at[there, part], to)
        ups, downs = ([C_DIAG + 4 * c + 2 * side + v for side in (0, 1)] for v in (0, 1))
        upward.extend(ups)
        downward.extend(downs)
        pl.when(has_up)(lambda: start_all(ups))
        pl.when(has_down)(lambda: start_all(downs))

    lane = lax.broadcasted_iota(jnp.int32, (8, COLS), 1)
    node = lax.broadcasted_iota(jnp.int32, (BLK, COLS), 0)

    def one_hots(blk):
        for r in range(2):
            local = jnp.broadcast_to(asg[blk, r : r + 1, :] & (BLK - 1), (8, COLS))
            for e in range(5):
                s = e - 2
                moved = pltpu.roll(local, (-s) % COLS, 1) if s else local
                if s < 0:
                    moved = jnp.where(lane < -s, -1, moved)
                if s > 0:
                    moved = jnp.where(lane >= COLS - s, -1, moved)
                tall = jnp.concatenate([moved] * (BLK // 8), axis=0)
                at = (r * 5 + e) * BLK
                hot[blk, at : at + BLK] = jnp.where(node == tall, 1.0, 0.0).astype(BF16)

    def iota(shape, dim):
        return lax.broadcasted_iota(jnp.int32, shape, dim)

    def ones_where(condition):
        return jnp.where(condition, 1.0, 0.0).astype(BF16)

    def inside(row):
        row = row + 2 * reg
        return jnp.logical_and(row >= 0, row < 2 * n_reg)

    def taps():
        return psi[...].reshape(50, NBAS).astype(BF16)

    def tap_matrices():
        spread = ones_where(iota((NBAS, NBAS * 16), 0) == iota((NBAS, NBAS * 16), 1) // 16)
        wide = jnp.dot(taps(), spread, preferred_element_type=F32).astype(BF16)
        line, tap = iota((320, 50), 0) // 16, iota((320, 50), 1)
        i, r, e = line // 10, (line // 5) % 2, line % 5
        diagonal = iota((320, NBAS * 16), 0) % 16 == iota((320, NBAS * 16), 1) % 16
        pick = ones_where(tap == ((r - i + 2) * 5 + e) * 2 + i)
        full = jnp.dot(pick, wide, preferred_element_type=F32)
        kron[...] = jnp.where(diagonal, full, 0.0).astype(BF16)

    def spread_taps():
        for n, (i, a) in enumerate(FAR):

            def at_step(e, _, n=n, i=i, a=a):
                for b in range(NBAS):
                    tap = jnp.where(inside(i + a), psi_s[a + 2, e, i, b], 0.0)
                    splat[(n * 5 + e) * NBAS + b] = jnp.full((16, 128), tap, F32).astype(BF16)
                return 0

            lax.fori_loop(0, 5, at_step, 0)

    def selections(blk):
        for i in range(2):
            taps_here = [
                (r, e, FAR.index((i, a)) * 5 + e)
                for r, a in ((r, 2 * (blk - 1) + r - i) for r in range(2))
                if (i, a) in FAR
                for e in range(5)
            ]

            def some(n, _, i=i, taps_here=taps_here):
                at = pl.multiple_of(n * 32, 32)
                hots = [hot[blk, pl.ds((r * 5 + e) * BLK + at, 32), :] for r, e, _ in taps_here]
                for b in range(NBAS):
                    total = None
                    for h, (_, _, k) in zip(hots, taps_here, strict=True):
                        tap = splat[k * NBAS + b]
                        tap = jnp.concatenate([tap, tap], axis=0)
                        tap = jnp.concatenate([tap, tap], axis=1)
                        total = tap * h if total is None else total + tap * h
                    sel[blk // 2, pl.ds(b * BLK + at, 32), pl.ds(i * COLS, COLS)] = total
                return 0

            lax.fori_loop(0, BLK // 32, some, 0)

    def halo_matrix():
        spread = ones_where(iota((NBAS * 16, NBAS), 0) // 16 == iota((NBAS * 16, NBAS), 1))
        tall = lax.dot_general(spread, taps(), NT, preferred_element_type=F32).astype(BF16)
        tap, column = iota((50, 1024), 0), iota((50, 1024), 1)
        i_t, a, e = tap % 2, tap // 10 - 2, (tap // 2) % 5 - 2
        to, cell = column // 128, column % 128
        i_out, out_col = to // 4, jnp.where(to % 4 < 2, to % 4, to % 4 + COLS - 4)
        within = cell % 16
        cell_row = jnp.where(cell < 16, 0, jnp.where(cell < 32, -2, 2)) + (within % 4) // 2
        cell_col = jnp.where(within < 4, COLS, -2) + within % 2
        real = jnp.logical_and(cell < 48, within < 8)
        match = jnp.logical_and(i_t == i_out, cell_row - i_out == a)
        match = jnp.logical_and(match, cell_col - out_col == e)
        match = jnp.logical_and(jnp.logical_and(match, real), inside(cell_row))
        every = jnp.dot(tall, ones_where(match), preferred_element_type=F32)
        line = iota((NBAS * 16, 128), 0) % 16
        mine = jnp.zeros((NBAS * 16, 128), F32)
        for to in range(8):
            mine = jnp.where(line == to, every[:, to * 128 : (to + 1) * 128], mine)
        for b in range(NBAS):
            hsel[:, b * 128 : (b + 1) * 128] = mine[b * 16 : (b + 1) * 16].astype(BF16)

    def keys_values(first, count, start=0, height=BLK):
        part = pl.ds(start, height)
        x = jnp.concatenate([slots[first + n, part] for n in range(count)], axis=0)
        kv = jnp.dot(x, wqkv[:, D:], preferred_element_type=F32).astype(BF16)
        for n in range(count):
            kb[CODE[first + n], part] = kv[n * height : (n + 1) * height, :D]
            vb[CODE[first + n], part] = kv[n * height : (n + 1) * height, D:]

    loads[3].wait()
    loads[4].wait()
    loads[9].wait()
    one_hots(1)
    tap_matrices()
    halo_matrix()
    spread_taps()
    relay(0)

    loads[5].wait()
    scale = math.log2(math.e) / math.sqrt(D // HEADS)
    projected = jnp.dot(slots[OWN], wqkv[...], preferred_element_type=F32)
    qb[...] = (projected[:, :D] * scale).astype(BF16)
    kb[CODE[OWN]] = projected[:, D : 2 * D].astype(BF16)
    vb[CODE[OWN]] = projected[:, 2 * D :].astype(BF16)

    relay(1)
    pl.when(has_down)(lambda: wait_all([C_AUP]))
    pl.when(has_up)(lambda: wait_all([C_ADOWN]))
    one_hots(0)
    one_hots(2)
    keys_values(LEFT, 2)
    pl.when(has_down)(lambda: wait_all([C_UP]))
    pl.when(has_up)(lambda: wait_all([C_DOWN]))
    keys_values(UP, 2)
    selections(0)
    selections(2)

    head_lane = iota((BLK, 128), 1) // 32
    zero = jnp.zeros((BLK, 128), BF16)

    def attend(part, keys, vals):
        q = qb[:, part]
        wide = jnp.concatenate([jnp.where(head_lane == h, q, zero) for h in range(4)], axis=0)
        scores = lax.dot_general(wide, keys, NT, preferred_element_type=F32)
        top = jnp.max(scores, axis=-1, keepdims=True)
        weights = jnp.exp2(scores - top).astype(BF16)
        ones = jnp.ones(vals.shape, BF16)
        summed = jnp.dot(
            weights, jnp.concatenate([vals, ones], axis=1), preferred_element_type=F32
        )
        num, den = summed[:BLK, :128], summed[:BLK, 128:]
        most = jnp.broadcast_to(top[:BLK], (BLK, 128))
        for h in range(1, 4):
            mine, rows = head_lane == h, slice(h * BLK, (h + 1) * BLK)
            num = jnp.where(mine, summed[rows, :128], num)
            den = jnp.where(mine, summed[rows, 128:], den)
            most = jnp.where(mine, top[rows], most)
        return num, den, most

    for g in range(4):
        part = pl.ds(g * 128, 128)
        own_num[:, part], own_den[:, part], own_top[:, part] = attend(
            part, kb[CODE[OWN], :, part], vb[CODE[OWN], :, part]
        )

    loads[6].wait()
    for o in range(OUTP // 16):
        for b in range(NBAS):
            piece = wdec[b, o * 16 : min(o * 16 + 16, OUT)]
            if piece.shape[0] < 16:
                piece = jnp.concatenate([piece, jnp.zeros((16 - piece.shape[0], D), BF16)], axis=0)
            at = (o * NBAS + b) * 16
            wtp[at : at + 16] = piece

    own = asg[1] & (BLK - 1)
    lane1 = lax.broadcasted_iota(jnp.int32, (8, 128), 1)
    marks = jnp.full((8, 128), -1, jnp.int32)
    for r in range(2):
        for side in range(2):
            piece = jnp.broadcast_to(own[r : r + 1, side * 128 : side * 128 + 128], (8, 128))
            first, source = 4 * side + 2 * r, 126 * side
            moved = pltpu.roll(piece, (first - source) % 128, 1) if first != source else piece
            marks = jnp.where(jnp.logical_and(lane1 >= first, lane1 < first + 2), moved, marks)
    tall = jnp.concatenate([marks] * (BLK // 8), axis=0)
    hits = jnp.where(node[:, :128] == tall, 1.0, 0.0)
    onehot_e[...] = jnp.transpose(hits)[:16].astype(BF16)

    for half in range(2):
        chunks = range(half * CHUNKS // 2, (half + 1) * CHUNKS // 2)
        from_down, from_up = (
            [C_DIAG + 4 * c + 2 * side + v for c in chunks for side in (0, 1)] for v in (0, 1)
        )
        pl.when(has_down)(lambda keys=from_down: wait_all(keys))
        pl.when(has_up)(lambda keys=from_up: wait_all(keys))
        keys_values(UL, 4, half * (BLK // 2), BLK // 2)

    slot = []
    for n in range(1, 5):
        there = nbr[0, n]
        row_step = there // n_lon - reg
        col_step = lax.rem(there % n_lon - lon + 1 + n_lon, n_lon) - 1
        code = (row_step + 1) * 3 + col_step + 1
        slot.append(jnp.clip(code, 0, 8))
    for g in range(4):
        part = pl.ds(g * 128, 128)
        keys = jnp.concatenate([kb[s, :, part] for s in slot], axis=0)
        vals = jnp.concatenate([vb[s, :, part] for s in slot], axis=0)
        num, den, top = attend(part, keys, vals)
        first = own_top[:, part]
        both = jnp.maximum(first, top)
        old, new = jnp.exp2(first - both), jnp.exp2(top - both)
        num = num * new + own_num[:, part] * old
        den = den * new + own_den[:, part] * old
        att[:, part] = (num / den).astype(BF16)

    loads[7].wait()
    loads[8].wait()
    state = (
        xs[...].astype(F32) + jnp.dot(att[...], wout[...], preferred_element_type=F32)
    ).astype(BF16)
    state_o[...] = state
    v = jnp.dot(state, wlat[...], preferred_element_type=F32)
    lat[1] = (v / (1.0 + jnp.exp(-v))).astype(BF16)

    edge[...] = jnp.dot(onehot_e[...], lat[1], preferred_element_type=F32).astype(BF16)
    for n, (to, there) in enumerate(zip([left, right, *corners], (0, 1, 4, 5, 2, 3), strict=True)):
        copies[C_EDGE + n] = remote(C_EDGE + n, edge, edges_in.at[there], to)
    copies[C_LUP] = remote(C_LUP, lat.at[1], lat.at[2], up)
    copies[C_LDOWN] = remote(C_LDOWN, lat.at[1], lat.at[0], down)
    start_all([C_EDGE, C_EDGE + 1])
    pl.when(has_up)(lambda: start_all([C_EDGE + 2, C_EDGE + 3, C_LUP]))
    pl.when(has_down)(lambda: start_all([C_EDGE + 4, C_EDGE + 5, C_LDOWN]))
    upward.extend([C_EDGE + 2, C_EDGE + 3, C_LUP])
    downward.extend([C_EDGE + 4, C_EDGE + 5, C_LDOWN])

    def mixed(nodes_in):
        return lax.dot_general(wtp[...], nodes_in, NT, preferred_element_type=F32).astype(BF16)

    n_out = OUTP // 16
    high = NBAS * 16

    def decode_own():
        z = mixed(lat[1])
        z = jnp.concatenate([z[o * high : (o + 1) * high] for o in range(n_out)], axis=1)
        w = jnp.dot(kron[...], z, preferred_element_type=F32).astype(BF16)
        pieces = []
        for i in range(2):
            for o in range(n_out):
                line = [w[(i * 10 + k) * 16 : (i * 10 + k + 1) * 16, o * 128 : (o + 1) * 128] for k in range(10)]
                pieces.append(jnp.concatenate(line, axis=1))
        return jnp.dot(jnp.concatenate(pieces, axis=0), hot[1], preferred_element_type=F32)

    def by_output(z):
        lines = [
            jnp.concatenate([z[o * high + b * 16 : o * high + b * 16 + 16] for b in range(NBAS)], axis=1)
            for o in range(n_out)
        ]
        return jnp.concatenate(lines, axis=0)

    def decode_far(z, k):
        return jnp.dot(by_output(z), sel[k], preferred_element_type=F32)

    total = decode_own()

    even = lax.rem(reg, 2) == 0
    has_far = jnp.logical_or(jnp.logical_and(even, has_up), jnp.logical_and(reg % 2 == 1, has_down))
    near = jnp.where(even, 1, 0)
    other[...] = jnp.zeros((OUTP, 2 * COLS), F32)

    def add_block(n, _):
        k = jnp.where(n == 0, near, 1 - near)

        @pl.when(jnp.logical_or(n == 0, has_far))
        def _():
            remote(C_LUP + 1 - k, lat.at[1], lat.at[k * 2], up).wait_recv()

        other[...] += decode_far(mixed(lat[k * 2]), k)
        return 0

    lax.fori_loop(0, 2, add_block, 0)
    wait_all([C_EDGE, C_EDGE + 1])
    pl.when(has_down)(lambda: wait_all([C_EDGE + 2, C_EDGE + 3]))
    pl.when(has_up)(lambda: wait_all([C_EDGE + 4, C_EDGE + 5]))
    first4 = iota((16, D), 0) < 4
    cells = []
    for n in range(3):
        a, b = edges_in[2 * n], edges_in[2 * n + 1]
        cells.append(jnp.where(first4, a, b))
    z = by_output(mixed(jnp.concatenate(cells + [jnp.zeros((80, D), BF16)], axis=0)))
    sides = lax.dot_general(z, hsel[...], NT, preferred_element_type=F32)
    sides = jnp.concatenate([sides, jnp.zeros((OUTP, 112), F32)], axis=1)
    lane2 = iota((OUTP, 128), 1)
    for i in range(2):
        at_left = pltpu.roll(sides, (-4 * i) % 128, 1) if i else sides
        at_left = jnp.where(lane2 < 2, at_left, 0.0)
        at_right = jnp.where(lane2 >= 126, pltpu.roll(sides, 124 - 4 * i, 1), 0.0)
        whole = total[i * OUTP : (i + 1) * OUTP] + other[:, i * COLS : (i + 1) * COLS]
        whole += jnp.concatenate([at_left, at_right], axis=1)
        fields_o[:, i, :] = whole[:OUT].astype(BF16)

    def sent(keys):
        for k in keys:
            copies[k].wait_send()

    sent([k for k in copies if k not in upward and k not in downward])
    pl.when(has_up)(lambda: sent(upward))
    pl.when(has_down)(lambda: sent(downward))


def store(state, fields, state_o, fields_o, sem):
    copies = [
        pltpu.make_async_copy(state, state_o, sem.at[0]),
        pltpu.make_async_copy(fields, fields_o, sem.at[1]),
    ]
    for copy in copies:
        copy.start()
    for copy in copies:
        copy.wait()


def shards(sizes, nodes, norm_gain, w_qkv, w_out, w_latent, neighbours, assignment, psi, w_dec):
    anywhere = pl.BlockSpec(memory_space=pl.ANY)
    vmem = pl.BlockSpec(memory_space=pltpu.VMEM)
    state, fields = pl.pallas_call(
        functools.partial(kernel, *sizes),
        out_shape=(
            pltpu.VMEM((BLK, D), BF16),
            pltpu.VMEM((OUT, 2, COLS), BF16),
        ),
        in_specs=[anywhere] * 9,
        out_specs=(vmem, vmem),
        scratch_shapes=[
            pltpu.VMEM((BLK, D), BF16),
            pltpu.VMEM((1, D), F32),
            pltpu.VMEM((D, 3 * D), BF16),
            pltpu.VMEM((D, D), BF16),
            pltpu.VMEM((D, D), BF16),
            pltpu.SMEM((1, 5), jnp.int32),
            pltpu.VMEM((3, 2, COLS), jnp.int32),
            pltpu.VMEM((5, 5, 2, NBAS), F32),
            pltpu.SMEM((5, 5, 2, NBAS), F32),
            pltpu.VMEM((NBAS, OUT, D), BF16),
            pltpu.VMEM((NBAS * OUTP, D), BF16),
            pltpu.VMEM((9, BLK, D), BF16),
            pltpu.VMEM((BLK, D), BF16),
            pltpu.VMEM((9, BLK, D), BF16),
            pltpu.VMEM((9, BLK, D), BF16),
            pltpu.VMEM((BLK, D), F32),
            pltpu.VMEM((BLK, D), F32),
            pltpu.VMEM((BLK, D), F32),
            pltpu.VMEM((BLK, D), BF16),
            pltpu.VMEM((3, BLK, D), BF16),
            pltpu.VMEM((16, D), BF16),
            pltpu.VMEM((6, 16, D), BF16),
            pltpu.VMEM((16, 128), BF16),
            pltpu.VMEM((3, 10 * BLK, COLS), BF16),
            pltpu.VMEM((320, NBAS * 16), BF16),
            pltpu.VMEM((16, NBAS * 128), BF16),
            pltpu.VMEM((30 * NBAS, 16, 128), BF16),
            pltpu.VMEM((2, NBAS * BLK, 2 * COLS), BF16),
            pltpu.VMEM((OUTP, 2 * COLS), F32),
            pltpu.SemaphoreType.DMA((10,)),
            pltpu.SemaphoreType.DMA((N_COPIES,)),
            pltpu.SemaphoreType.DMA((N_COPIES,)),
        ],
        compiler_params=pltpu.CompilerParams(
            collective_id=0, has_side_effects=True, vmem_limit_bytes=56 * 2**20
        ),
    )(
        nodes[0], norm_gain[None], w_qkv, w_out, w_latent, neighbours, assignment,
        psi.transpose(2, 3, 1, 0), w_dec.transpose(0, 2, 1),
    )
    state, fields = pl.pallas_call(
        store,
        out_shape=(
            jax.ShapeDtypeStruct((BLK, D), BF16),
            jax.ShapeDtypeStruct((OUT, 2, COLS), BF16),
        ),
        in_specs=[vmem] * 2,
        out_specs=(anywhere, anywhere),
        scratch_shapes=[pltpu.SemaphoreType.DMA((2,))],
    )(
        pltpu.with_memory_space_constraint(state, pltpu.VMEM),
        pltpu.with_memory_space_constraint(fields, pltpu.VMEM),
    )
    return state[None], fields[None]


def solution(mesh):
    sizes = (mesh.shape["reg"], mesh.shape["lon"])
    in_specs = (
        P(None, ("reg", "lon"), None),
        P(),
        P(),
        P(),
        P(),
        P(("reg", "lon"), None),
        P("reg", "lon"),
        P(None, "reg", None, None),
        P(),
    )
    out_specs = (P(None, ("reg", "lon"), None), P(None, None, "reg", "lon"))
    return jax.shard_map(
        functools.partial(shards, sizes),
        mesh=mesh,
        in_specs=in_specs,
        out_specs=out_specs,
        check_vma=False,
    )
```
